128 devices in a mesh: img: 16 (over z_hi, x, core), ori: 8 (over z_lo, y).
Axes of the slice: x: 4, y: 4, z: 4 (z_hi: 2, z_lo: 2; z = z_hi * 2 + z_lo), core: 2. Of those that a mesh axis runs over, the one named last changes fastest.
Arguments:
- images: bfloat16 [4096, 32768], P('img')
- classes: int32 [4096], P('img'), may hold values from 0 to 31
- contrast: float32 [32, 16384], replicated, may hold values from 0.1 to 1
- noise_weight: float32 [16384], replicated, may hold values from 0.5 to 2
- projections: bfloat16 [8, 192, 32768], P('ori', 'img')
- proj_index: int32 [4096], P('ori'), may hold values from 0 to 191, as said below
Outputs:
- log_weights: float32 [4096, 4096], P('img', 'ori')
- back_sums: bfloat16 [8, 192, 32768], P('ori', 'img')
- contrast_mass: float32 [8, 192, 16384], P('ori', 'img')
The draws below stay inside these ranges and needn't reach their ends.
Inputs may be any that keep to these rules, and one draw needn't show every extreme that they name: proj_index[j] names a projection of orientation block j // 512; every one of a block's 192 projections is named by at least one orientation of that block.
All inputs are finite; a program needn't handle non-finite values.
Results may differ from the reference program's by a relative error of at most 0.017.
Values may be sent and summed in bfloat16 or wider, within the bound.
No kernel may reach another device: no remote copies, remote signals or barrier semaphores. Data moves between devices by JAX's collectives and lax.ppermute only.
A program may use at most 320 MiB of HBM per device.

```python
import math
import jax
import jax.numpy as jnp
from jax import lax

COEFFS = 16384
CLASSES = 32
ORI_DEV = 512
NIMG = 4096
BLOCKS = 8
PROJ_BLK = 192
N_IMG = 16


def common_direction(key):
    return jax.random.normal(jax.random.fold_in(key, 13), (2 * COEFFS,), jnp.float32)


def projection_base(key):
    noise_key = jax.random.fold_in(key, 11)
    scale_key = jax.random.fold_in(key, 12)
    noise = jax.random.normal(noise_key, (BLOCKS, PROJ_BLK, 2 * COEFFS), jnp.float32)
    scales = jnp.exp(jax.random.uniform(scale_key, (BLOCKS, PROJ_BLK, 1), jnp.float32, math.log(0.7), math.log(1.4)))
    tilt = (jnp.arange(BLOCKS, dtype=jnp.float32) / max(BLOCKS - 1, 1)).reshape(BLOCKS, 1, 1)
    shared = common_direction(key).reshape(1, 1, 2 * COEFFS)
    return 2.0 / math.sqrt(COEFFS) * scales * (noise + tilt * shared)


def draw_projections(key, part):
    return projection_base(key).astype(jnp.bfloat16)


def image_values(key, lift, stride, low_strength, high_strength):
    shared = projection_base(key).reshape(BLOCKS * PROJ_BLK, 2 * COEFFS)
    direction = common_direction(key)
    key = jax.random.fold_in(key, 3)
    noise = jax.random.normal(jax.random.fold_in(key, 1), (NIMG, 2 * COEFFS), jnp.float32)
    first_pick = jax.random.randint(jax.random.fold_in(key, 4), (NIMG,), 0, BLOCKS * PROJ_BLK)
    second_pick = jax.random.randint(jax.random.fold_in(key, 5), (NIMG,), 0, BLOCKS * PROJ_BLK)
    strength = jnp.exp(jax.random.uniform(jax.random.fold_in(key, 6), (NIMG, 1), jnp.float32, math.log(low_strength), math.log(high_strength)))
    aligned = (jnp.arange(NIMG) % stride == 0)[:, None]
    mixed = strength * (shared[first_pick] + 0.9 * shared[second_pick]) + 0.3 * noise
    drawn = noise
    lifted = lift / math.sqrt(COEFFS) * direction[None, :]
    return jnp.where(aligned, mixed, drawn) + lifted


def draw_images(key, part):
    values = image_values(key, 1.5, 16, 40.0, 160.0)
    return values.astype(jnp.bfloat16)


def draw_proj_index(key, part):
    key = jax.random.fold_in(key, 7)
    block_keys = jax.random.split(key, BLOCKS)

    def one_block(block_key):
        order = jax.random.permutation(jax.random.fold_in(block_key, 1), ORI_DEV)
        spare = jax.random.randint(jax.random.fold_in(block_key, 2), (ORI_DEV,), 0, PROJ_BLK)
        return jnp.where(order < PROJ_BLK, order, spare)
    return jax.vmap(one_block)(block_keys).reshape(-1).astype(jnp.int32)


def plant(array, rng, low, largest):
    spot = [jax.random.randint(jax.random.fold_in(rng, axis), (), 0, length) for axis, length in enumerate(array.shape)]
    widest = array.shape.index(max(array.shape))
    beside = spot[:widest] + [(spot[widest] + 1) % array.shape[widest]] + spot[widest + 1:]
    return array.at[tuple(spot)].set(low).at[tuple(beside)].set(largest)


def setup_inputs(seed: int = 0) -> dict:
    keys = jax.random.split(jax.random.key(seed), 7)
    images = draw_images(jax.random.fold_in(keys[6], 71), 0)
    classes = plant(jax.random.randint(keys[1], (NIMG,), 0, CLASSES), jax.random.fold_in(keys[1], 1), 0, CLASSES - 1).astype(jnp.int32)
    contrast = jnp.clip(jax.random.uniform(keys[2], (CLASSES, COEFFS), jnp.float32, 0.1, 1.0), 0.1, 1.0)
    noise_weight = jnp.clip(jnp.exp(jax.random.uniform(keys[3], (COEFFS,), jnp.float32, math.log(0.5), math.log(2.0))), 0.5, 2.0)
    projections = draw_projections(jax.random.fold_in(keys[6], 71), 0)
    proj_index = draw_proj_index(jax.random.fold_in(keys[6], 71), 0)
    return {"images": images, "classes": classes, "contrast": contrast, "noise_weight": noise_weight, "projections": projections, "proj_index": proj_index}


PRECISE = lax.Precision.HIGHEST


def reference(images, classes, contrast, noise_weight, projections, proj_index):
    img_total = images.shape[0]
    half_len = contrast.shape[1]
    class_count = contrast.shape[0]
    block_count = projections.shape[0]
    block_width = projections.shape[1]
    per_block = proj_index.shape[0] // block_count
    group_rows = img_total // N_IMG
    class_hot = (classes[:, None] == jnp.arange(class_count, dtype=jnp.int32)[None, :]).astype(jnp.float32)
    amplitude = (contrast * noise_weight[None, :])[classes]
    weighted = (images.astype(jnp.float32).reshape(img_total, 2, half_len) * amplitude[:, None, :]).reshape(img_total, 2 * half_len).astype(jnp.bfloat16)
    half_quad = 0.5 * contrast * contrast * noise_weight[None, :]
    squared = contrast * contrast
    score_list = []
    for section in range(block_count):
        slab_rows = projections[section]
        correl = lax.dot_general(weighted, slab_rows, (((1,), (1,)), ((), ())), preferred_element_type=jnp.float32)
        power = jnp.sum(jnp.square(slab_rows.astype(jnp.float32).reshape(block_width, 2, half_len)), axis=1)
        quad_part = lax.dot_general(half_quad, power, (((1,), (1,)), ((), ())), precision=PRECISE)
        indices = proj_index[section * per_block:(section + 1) * per_block]
        score_list.append((correl - quad_part[classes])[:, indices])
    scores = jnp.concatenate(score_list, axis=1)
    highest = jnp.max(scores, axis=1)
    summed = jnp.sum(jnp.exp(scores - highest[:, None]), axis=1)
    log_weights = scores - (highest + jnp.log(summed))[:, None]
    chances = jnp.exp(log_weights).astype(jnp.bfloat16)
    back_list = []
    mass_list = []
    for section in range(block_count):
        indices = proj_index[section * per_block:(section + 1) * per_block]
        choose = (jnp.arange(block_width, dtype=jnp.int32)[:, None] == indices[None, :]).astype(jnp.bfloat16)
        per_proj = lax.dot_general(chances[:, section * per_block:(section + 1) * per_block], choose, (((1,), (1,)), ((), ())), preferred_element_type=jnp.float32).astype(jnp.bfloat16)

        def add_group(cohort, accum):
            first_row = (cohort * group_rows).astype(jnp.int32)
            group_probs = lax.dynamic_slice_in_dim(per_proj, first_row, group_rows, 0)
            group_images = lax.dynamic_slice_in_dim(weighted, first_row, group_rows, 0)
            partial_sum = lax.dot_general(group_probs, group_images, (((0,), (0,)), ((), ())), preferred_element_type=jnp.float32)
            return accum + lax.optimization_barrier(partial_sum.astype(jnp.bfloat16)).astype(jnp.float32)

        accum = lax.fori_loop(0, N_IMG, add_group, jnp.zeros((block_width, 2 * half_len), jnp.float32))
        back_list.append(accum.astype(jnp.bfloat16))
        class_totals = lax.dot_general(per_proj.astype(jnp.float32), class_hot, (((0,), (0,)), ((), ())), precision=PRECISE)
        mass_list.append(jnp.dot(class_totals, squared, precision=PRECISE))
    return log_weights, jnp.stack(back_list), jnp.stack(mass_list)
```

```python
import functools

import jax
import jax.numpy as jnp
from jax import lax
from jax.experimental import pallas as pl
from jax.experimental.pallas import tpu as pltpu
from jax.sharding import PartitionSpec as P

PRECISE = lax.Precision.HIGHEST
F32 = jnp.float32
BF16 = jnp.bfloat16
NX, NC = 4, 2
TAIL = 128
NT = (((1,), (1,)), ((), ()))
NN = (((1,), (0,)), ((), ()))
VMEM_LIMIT = 48 * 1024 * 1024


def img_perm(dz, dx, dc):
    pairs = []
    for z in range(2):
        for x in range(NX):
            for c in range(NC):
                src = (z * NX + x) * NC + c
                dst = ((z ^ dz) * NX + (x + dx) % NX) * NC + (c ^ dc)
                pairs.append((src, dst))
    return pairs


def ori_perm(dz, dy):
    return [(z * 4 + y, (z ^ dz) * 4 + (y + dy) % 4) for z in range(2) for y in range(4)]


def to_xp(v):
    return lax.ppermute(v, "img", img_perm(0, 1, 0))


def to_xm(v):
    return lax.ppermute(v, "img", img_perm(0, -1, 0))


def to_z(v):
    return lax.ppermute(v, "img", img_perm(1, 0, 0))


def to_core(v):
    return lax.ppermute(v, "img", img_perm(0, 0, 1))


def params(n=1):
    return pltpu.CompilerParams(
        dimension_semantics=("arbitrary",) * n, vmem_limit_bytes=VMEM_LIMIT
    )


def full(shape):
    return pl.BlockSpec(shape, lambda j: (0,) * len(shape))


def weigh_kernel(core, keep_img, give_img, hot3, contrast, noise, keep_out, give_out):
    amp = contrast[...] * noise[...]
    a1 = amp.astype(BF16)
    rest = amp - a1.astype(F32)
    a2 = rest.astype(BF16)
    a3 = (rest - a2.astype(F32)).astype(BF16)
    table = jnp.concatenate([a1, a2, a3], axis=0)
    amplitude = lax.dot_general(hot3[...], table, NN, preferred_element_type=F32)
    give_out[...] = (give_img[...].astype(F32) * amplitude).astype(BF16)
    keep_out[...] = (keep_img[...].astype(F32) * amplitude).astype(BF16)


def weigh(core, images, hot3, contrast, noise):
    rows, cols = images.shape
    half = cols // 2
    kb = 1024
    nb = half // kb
    classes = contrast.shape[0]
    return pl.pallas_call(
        weigh_kernel,
        grid_spec=pltpu.PrefetchScalarGridSpec(
            num_scalar_prefetch=1,
            grid=(nb,),
            in_specs=[
                pl.BlockSpec((rows, kb), lambda j, s: (0, s[0] * nb + j)),
                pl.BlockSpec((rows, kb), lambda j, s: (0, (1 - s[0]) * nb + j)),
                pl.BlockSpec(hot3.shape, lambda j, s: (0, 0)),
                pl.BlockSpec((classes, kb), lambda j, s: (0, j)),
                pl.BlockSpec((1, kb), lambda j, s: (0, j)),
            ],
            out_specs=[
                pl.BlockSpec((rows, kb), lambda j, s: (0, j)),
                pl.BlockSpec((rows, kb), lambda j, s: (0, j)),
            ],
        ),
        out_shape=[jax.ShapeDtypeStruct((rows, half), BF16)] * 2,
        compiler_params=params(),
        cost_estimate=pl.CostEstimate(
            flops=2 * rows * 96 * half, bytes_accessed=8 * rows * half, transcendentals=0
        ),
        name="weigh",
    )(core, images, images, hot3, contrast, noise)


def score_kernel(n_parts, has_acc, nb, *refs):
    parts = refs[:n_parts]
    w_own, w_sib, contrast, noise, hot = refs[n_parts : n_parts + 5]
    pos = n_parts + 5
    acc_in = refs[pos] if has_acc else None
    out, acc, qacc = refs[pos + has_acc :]
    j = pl.program_id(0)

    @pl.when(j == 0)
    def _():
        acc[...] = jnp.zeros_like(acc)
        qacc[...] = jnp.zeros_like(qacc)

    pieces = [r[...].astype(F32) for r in parts]
    used = sum(p.shape[0] for p in pieces)
    pieces.append(jnp.zeros((128 - used, pieces[0].shape[1]), F32))
    p32 = jnp.concatenate(pieces, axis=0)
    pb = p32.astype(BF16)
    rows = w_own.shape[0]
    acc[:rows, :] += lax.dot_general(w_own[...], pb, NT, preferred_element_type=F32)
    acc[rows:, :] += lax.dot_general(w_sib[...], pb, NT, preferred_element_type=F32)
    sq = p32 * p32
    hi = sq.astype(BF16)
    lo = (sq - hi.astype(F32)).astype(BF16)
    hq = 0.5 * contrast[...] * contrast[...] * noise[...]
    h1 = hq.astype(BF16)
    h2 = (hq - h1.astype(F32)).astype(BF16)
    hh = jnp.concatenate([h1, h2], axis=0)
    qacc[...] += lax.dot_general(hh, hi, NT, preferred_element_type=F32) + lax.dot_general(
        hh, lo, NT, preferred_element_type=F32
    )

    @pl.when(j == nb - 1)
    def _():
        n_cls = h1.shape[0]
        quad = qacc[:n_cls, :] + qacc[n_cls:, :]
        total = acc[...] - jnp.dot(hot[...], quad, precision=PRECISE, preferred_element_type=F32)
        turned = jnp.transpose(total)[:used, :]
        if has_acc:
            turned = turned + acc_in[...]
        out[...] = turned


def score(parts, w_own, w_sib, contrast, noise, hot, quarter, acc_in):
    part_rows, q = parts[0].shape
    rows = w_own.shape[0]
    n_cls = contrast.shape[0]
    kb = 1024
    nb = q // kb
    used = part_rows * len(parts)
    off = quarter * nb
    in_specs = [pl.BlockSpec((part_rows, kb), lambda j: (0, j)) for _ in parts]
    in_specs += [
        pl.BlockSpec((rows, kb), lambda j: (0, off + j)),
        pl.BlockSpec((rows, kb), lambda j: (0, off + j)),
        pl.BlockSpec((n_cls, kb), lambda j: (0, off + j)),
        pl.BlockSpec((1, kb), lambda j: (0, off + j)),
        full(hot.shape),
    ]
    args = [*parts, w_own, w_sib, contrast, noise, hot]
    if acc_in is not None:
        in_specs.append(full((used, 2 * rows)))
        args.append(acc_in)
    return pl.pallas_call(
        functools.partial(score_kernel, len(parts), acc_in is not None, nb),
        grid=(nb,),
        in_specs=in_specs,
        out_specs=full((used, 2 * rows)),
        out_shape=jax.ShapeDtypeStruct((used, 2 * rows), F32),
        scratch_shapes=[
            pltpu.VMEM((2 * rows, 128), F32),
            pltpu.VMEM((2 * n_cls, 128), F32),
        ],
        compiler_params=params(),
        cost_estimate=pl.CostEstimate(
            flops=2 * 2 * rows * 256 * q, bytes_accessed=4 * rows * q, transcendentals=0
        ),
        name="score",
    )(*args)


def stat_kernel(am, ar, bm, br, cnt_a, cnt_b, a_out, b_out, st_out):
    rows = am.shape[1] // 2

    def both(mine, recv):
        r = recv[...]
        return mine[...] + jnp.concatenate([r[:, rows:], r[:, :rows]], axis=1)

    a = both(am, ar)
    b = both(bm, br)
    a_out[...] = a
    b_out[...] = b
    peak = jnp.maximum(jnp.max(a, axis=0, keepdims=True), jnp.max(b, axis=0, keepdims=True))
    mass = jnp.sum(jnp.exp(a - peak) * cnt_a[...], axis=0, keepdims=True) + jnp.sum(
        jnp.exp(b - peak) * cnt_b[...], axis=0, keepdims=True
    )
    st_out[0:1, :] = peak
    st_out[1:2, :] = mass


def chance_kernel(n, *refs):
    a, b, cnt_a, cnt_b, hot = refs[:5]
    stats = refs[5 : 5 + n]
    pa, pb, la, lb, ta, tb = refs[5 + n :]
    peak = stats[0][0:1, :]
    for s in stats[1:]:
        peak = jnp.maximum(peak, s[0:1, :])
    mass = jnp.zeros_like(peak)
    for s in stats:
        mass = mass + s[1:2, :] * jnp.exp(s[0:1, :] - peak)
    shift = peak + jnp.log(mass)
    own = la.shape[1]
    for src, cnt, p_out, l_out, t_out in ((a, cnt_a, pa, la, ta), (b, cnt_b, pb, lb, tb)):
        lw = src[...] - shift
        l_out[...] = lw[:, :own]
        chance = jnp.exp(lw).astype(BF16).astype(F32)
        per = (chance * cnt[...]).astype(BF16)
        p_out[...] = per
        tot = jnp.dot(per, hot[...], preferred_element_type=F32)
        hi = tot.astype(BF16).astype(F32)
        t_out[...] = hi + pltpu.roll(tot - hi, 32, 1)


def whole(kernel, out_shape, name, *args):
    return pl.pallas_call(
        kernel,
        out_shape=out_shape,
        compiler_params=pltpu.CompilerParams(vmem_limit_bytes=VMEM_LIMIT),
        name=name,
    )(*args)


def back_kernel(n_parts, nb, kb, tail, *refs):
    pa, pb, w_own, w_sib, ta, tb = refs[:6]
    outs = refs[6:]
    j = pl.program_id(0)
    per = jnp.concatenate([pa[...], pb[...]], axis=0)
    rows = w_own.shape[0]
    res = lax.dot_general(
        per[:, :rows], w_own[...], NN, preferred_element_type=F32
    ) + lax.dot_general(per[:, rows:], w_sib[...], NN, preferred_element_type=F32)
    h = per.shape[0] // n_parts
    at = pl.ds(pl.multiple_of(j * kb, kb), kb)
    for i, o in enumerate(outs):
        o[:, at] = res[i * h : (i + 1) * h, :].astype(BF16)
    if tail:

        @pl.when(j == nb - 1)
        def _():
            tot = jnp.concatenate([ta[...], tb[...]], axis=0)
            for i, o in enumerate(outs):
                o[:, nb * kb :] = tot[i * h : (i + 1) * h, :].astype(BF16)


def back(pa, pb, w_own, w_sib, ta, tb, quarter, n_parts, tail):
    rows, half = w_own.shape
    q = half // 2
    kb = 1024
    nb = q // kb
    off = quarter * nb
    h = (pa.shape[0] + pb.shape[0]) // n_parts
    width = q + (TAIL if tail else 0)
    return pl.pallas_call(
        functools.partial(back_kernel, n_parts, nb, kb, tail),
        grid=(nb,),
        in_specs=[
            full(pa.shape),
            full(pb.shape),
            pl.BlockSpec((rows, kb), lambda j: (0, off + j)),
            pl.BlockSpec((rows, kb), lambda j: (0, off + j)),
            full(ta.shape),
            full(tb.shape),
        ],
        out_specs=[full((h, width))] * n_parts,
        out_shape=[jax.ShapeDtypeStruct((h, width), BF16)] * n_parts,
        compiler_params=params(),
        cost_estimate=pl.CostEstimate(
            flops=2 * 2 * rows * 256 * q, bytes_accessed=4 * rows * q, transcendentals=0
        ),
        name="back",
    )(pa, pb, w_own, w_sib, ta, tb)


def add_tail(tail):
    tot = tail + pltpu.roll(tail, TAIL - 32, 1)
    lane = lax.broadcasted_iota(jnp.int32, tail.shape, 1)
    tot = jnp.where(lane < 32, tot, 0.0)
    hi = tot.astype(BF16).astype(F32)
    return hi + pltpu.roll(tot - hi, 32, 1)


def add_kernel(n, tail, *refs):
    out = refs[n]
    width = out.shape[1] - (TAIL if tail else 0)
    total = refs[0][...].astype(F32)
    for r in refs[1:n]:
        total = total + r[...].astype(F32)
    if tail:
        out[:, :width] = total[:, :width].astype(BF16)
        out[:, width:] = add_tail(total[:, width:]).astype(BF16)
    else:
        out[...] = total.astype(BF16)


def add(*arrays, tail):
    return whole(
        functools.partial(add_kernel, len(arrays), tail),
        jax.ShapeDtypeStruct(arrays[0].shape, BF16),
        "add",
        *arrays,
    )


def tie(value, *others):
    return lax.optimization_barrier((value, *others))[0]


def shards(images, classes, contrast, noise_weight, projections, proj_index):
    half = contrast.shape[1]
    quart = half // 2
    n_cls = contrast.shape[0]
    own_rows = projections.shape[1]
    h = 2 * own_rows
    me = lax.axis_index("img")
    core = (me % NC).astype(jnp.int32)
    chip = (me // NC).astype(jnp.int32)
    first = core == 0
    noise = noise_weight[None, :]

    mine = projections[0]
    low, high = mine[:, :half], mine[:, half:]
    got = to_core(jnp.where(first, high, low))
    kept = jnp.where(first, low, high)
    shard = jnp.where(
        first, jnp.concatenate([kept, got], axis=0), jnp.concatenate([got, kept], axis=0)
    )
    own = [shard[:, :quart], shard[:, quart:]]

    xm_a, xp_a, zz_a = to_xp(own[0]), to_xm(own[0]), to_z(own[0])
    xm_b, xp_b, zz_b = to_xp(own[1]), to_xm(own[1]), to_z(own[1])
    x2_a, x2_b = to_xp(xm_a), to_xm(xp_b)
    zz_a2, zz_b2 = tie(zz_a, x2_a, x2_b), tie(zz_b, x2_a, x2_b)
    zm_a, zp_a, z2_a = to_xp(zz_a2), to_xm(zz_a2), to_z(x2_a)
    zm_b, zp_b, z2_b = to_xp(zz_b2), to_xm(zz_b2), to_z(x2_b)

    sib_classes = to_core(classes)
    ids = jnp.arange(n_cls, dtype=jnp.int32)[None, :]
    hot_own = (classes[:, None] == ids).astype(BF16)
    both_classes = jnp.concatenate([classes, sib_classes])
    hot = (both_classes[:, None] == ids).astype(F32)
    hot_wide = (both_classes[:, None] == jnp.arange(TAIL, dtype=jnp.int32)[None, :]).astype(BF16)
    hot3 = jnp.concatenate([hot_own] * 3, axis=1)
    w_own, w_give = weigh(core.reshape(1), images, hot3, contrast, noise)
    w_sib = to_core(w_give)

    target = proj_index // h
    dz = (target // NX) ^ (chip // NX)
    dx = (target - chip) % NX
    near = jnp.where(dx == 0, 0, jnp.where(dx == 1, 1, jnp.where(dx == 3, 2, 4)))
    far = jnp.where(dx == 0, 3, jnp.where(dx == 1, 5, jnp.where(dx == 3, 6, 7)))
    rel = jnp.where(dz == 0, near, far) * h + proj_index % h
    block_width = 8 * h
    choose = (jnp.arange(block_width, dtype=jnp.int32)[:, None] == rel[None, :]).astype(F32)
    counts = jnp.sum(choose, axis=1, keepdims=True)
    cnt_a, cnt_b = counts[: 4 * h], counts[4 * h :]

    table = (contrast, noise, hot)
    sa = score([own[0], xp_a, xm_a, zz_a], w_own, w_sib, *table, 0, None)
    sa = score([own[1], xp_b, xm_b, zz_b], w_own, w_sib, *table, 1, sa)
    sb = score([x2_a, zp_a, zm_a, z2_a], w_own, w_sib, *table, 0, None)
    sb = score([x2_b, zp_b, zm_b, z2_b], w_own, w_sib, *table, 1, sb)
    ra, rb = to_core(sa), to_core(sb)
    group = jax.ShapeDtypeStruct(sa.shape, F32)
    stat_shape = jax.ShapeDtypeStruct((2, sa.shape[1]), F32)
    ta, tb, stat = whole(
        stat_kernel, [group, group, stat_shape], "stat", sa, ra, sb, rb, cnt_a, cnt_b
    )
    stats = [stat]
    for z in range(2):
        for y in range(4):
            if z or y:
                stats.append(lax.ppermute(stat, "ori", ori_perm(z, y)))
    per_shape = jax.ShapeDtypeStruct(sa.shape, BF16)
    lw_shape = jax.ShapeDtypeStruct((sa.shape[0], sa.shape[1] // 2), F32)
    tot_shape = jax.ShapeDtypeStruct((sa.shape[0], TAIL), F32)
    pa, pb, la, lb, tot_a, tot_b = whole(
        functools.partial(chance_kernel, len(stats)),
        [per_shape, per_shape, lw_shape, lw_shape, tot_shape, tot_shape],
        "chance",
        ta,
        tb,
        cnt_a,
        cnt_b,
        hot_wide,
        *stats,
    )
    log_weights = lax.dot_general(
        jnp.concatenate([la, lb], axis=0), choose, (((0,), (0,)), ((), ())), precision=PRECISE
    )

    bo_a, bxp_a, bxm_a, bzz_a, bx2_a, bzp_a, bzm_a, bz2_a = back(
        pa, pb, w_own, w_sib, tot_a, tot_b, 0, 8, True
    )
    bo_b, bxp_b, bxm_b, bzz_b, bx2_b, bzp_b, bzm_b, bz2_b = back(
        pa, pb, w_own, w_sib, tot_a, tot_b, 1, 8, False
    )
    r_z2a, r_zma, r_zpa = to_z(bz2_a), to_xm(bzm_a), to_xp(bzp_a)
    r_z2b, r_zmb, r_zpb = to_z(bz2_b), to_xm(bzm_b), to_xp(bzp_b)
    r_x2a = to_xm(add(bx2_a, r_z2a, tail=True))
    r_x2b = to_xp(add(bx2_b, r_z2b, tail=False))
    r_zza = to_z(add(bzz_a, r_zma, r_zpa, tail=True))
    r_zzb = to_z(add(bzz_b, r_zmb, r_zpb, tail=False))
    r_xpa, r_xmb = to_xp(bxp_a), to_xm(bxm_b)
    r_xma = to_xm(add(bxm_a, r_x2a, tail=True))
    r_xpb = to_xp(add(bxp_b, r_x2b, tail=False))
    fin_a = add(bo_a, r_xpa, r_xma, r_zza, tail=True)
    fin_b = add(bo_b, r_xpb, r_xmb, r_zzb, tail=False)

    fin = jnp.concatenate([fin_a[:, :quart], fin_b], axis=1)
    got = to_core(jnp.where(first, fin[own_rows:], fin[:own_rows]))
    kept = jnp.where(first, fin[:own_rows], fin[own_rows:])
    back_sums = jnp.where(
        first, jnp.concatenate([kept, got], axis=1), jnp.concatenate([got, kept], axis=1)
    )
    ends = fin_a[:, quart:].astype(F32)
    totals = ends[:, :n_cls] + ends[:, n_cls : 2 * n_cls]
    totals = jnp.where(first, totals[:own_rows], totals[own_rows:])
    contrast_mass = jnp.dot(totals, contrast * contrast, precision=PRECISE)
    return log_weights, back_sums[None], contrast_mass[None]


def solution(mesh):
    in_specs = (P("img", None), P("img"), P(), P(), P("ori", "img", None), P("ori"))
    out_specs = (P("img", "ori"), P("ori", "img", None), P("ori", "img", None))
    return jax.shard_map(shards, mesh=mesh, in_specs=in_specs, out_specs=out_specs, check_vma=False)
```

```python
import functools

import jax
import jax.numpy as jnp
from jax import lax
from jax.experimental import pallas as pl
from jax.experimental.pallas import tpu as pltpu
from jax.sharding import PartitionSpec as P

PRECISE = lax.Precision.HIGHEST
F32 = jnp.float32
BF16 = jnp.bfloat16
NX, NC = 4, 2
TAIL = 128
LANES = 256
KB = 1024
CHEAP = pl.CostEstimate(flops=1024, bytes_accessed=1024, transcendentals=0)
NT = (((1,), (1,)), ((), ()))
NN = (((1,), (0,)), ((), ()))
VMEM_LIMIT = 48 * 1024 * 1024


def img_perm(dz, dx, dc):
    pairs = []
    for z in range(2):
        for x in range(NX):
            for c in range(NC):
                src = (z * NX + x) * NC + c
                dst = ((z ^ dz) * NX + (x + dx) % NX) * NC + (c ^ dc)
                pairs.append((src, dst))
    return pairs


def ori_perm(dz, dy):
    return [(z * 4 + y, (z ^ dz) * 4 + (y + dy) % 4) for z in range(2) for y in range(4)]


def to_xp(v):
    return lax.ppermute(v, "img", img_perm(0, 1, 0))


def to_xm(v):
    return lax.ppermute(v, "img", img_perm(0, -1, 0))


def to_z(v):
    return lax.ppermute(v, "img", img_perm(1, 0, 0))


def to_core(v):
    return lax.ppermute(v, "img", img_perm(0, 0, 1))


def params(mib=48):
    return pltpu.CompilerParams(
        dimension_semantics=("arbitrary",), vmem_limit_bytes=mib * 1024 * 1024
    )


def full(shape):
    return pl.BlockSpec(shape, lambda j: (0,) * len(shape))


def weigh_kernel(core, keep, give, hot3, contrast, noise, keep_out, give_out):
    amp = contrast[...] * noise[...]
    a1 = amp.astype(BF16)
    rest = amp - a1.astype(F32)
    a2 = rest.astype(BF16)
    a3 = (rest - a2.astype(F32)).astype(BF16)
    table = jnp.concatenate([a1, a2, a3], axis=0)
    amplitude = lax.dot_general(hot3[...], table, NN, preferred_element_type=F32)
    for img, out in ((give, give_out), (keep, keep_out)):
        value = (img[...].astype(F32) * amplitude).astype(BF16)
        for i in range(out.shape[0]):
            out[i] = value[:, i * KB : (i + 1) * KB]


def weigh(core, images, hot3, contrast, noise, quarter):
    rows, cols = images.shape
    half = cols // 2
    wide = 4
    kb = wide * KB
    nb = half // kb
    n_cls = contrast.shape[0]
    off = quarter * nb // 2
    return pl.pallas_call(
        weigh_kernel,
        grid_spec=pltpu.PrefetchScalarGridSpec(
            num_scalar_prefetch=1,
            grid=(nb // 2,),
            in_specs=[
                pl.BlockSpec((rows, kb), lambda j, s: (0, s[0] * nb + off + j)),
                pl.BlockSpec((rows, kb), lambda j, s: (0, (1 - s[0]) * nb + off + j)),
                pl.BlockSpec(hot3.shape, lambda j, s: (0, 0)),
                pl.BlockSpec((n_cls, kb), lambda j, s: (0, off + j)),
                pl.BlockSpec((1, kb), lambda j, s: (0, off + j)),
            ],
            out_specs=[pl.BlockSpec((wide, rows, KB), lambda j, s: (j, 0, 0))] * 2,
        ),
        out_shape=[jax.ShapeDtypeStruct((half // KB // 2, rows, KB), BF16)] * 2,
        compiler_params=params(),
        cost_estimate=CHEAP,
        name="weigh",
    )(core, images, images, hot3, contrast, noise)


def table_kernel(contrast, noise, out):
    hq = 0.5 * contrast[...] * contrast[...] * noise[...]
    h1 = hq.astype(BF16)
    h2 = (hq - h1.astype(F32)).astype(BF16)
    out[...] = jnp.concatenate([h1, h2], axis=0)


def quad_table(contrast, noise):
    n_cls, half = contrast.shape
    kb = 4 * KB
    return pl.pallas_call(
        table_kernel,
        grid=(half // kb,),
        in_specs=[
            pl.BlockSpec((n_cls, kb), lambda j: (0, j)),
            pl.BlockSpec((1, kb), lambda j: (0, j)),
        ],
        out_specs=pl.BlockSpec((2 * n_cls, kb), lambda j: (0, j)),
        out_shape=jax.ShapeDtypeStruct((2 * n_cls, half), BF16),
        compiler_params=params(),
        cost_estimate=CHEAP,
        name="table",
    )(contrast, noise)


def score_kernel(n_parts, has_acc, nb, wide, *refs):
    parts = refs[:n_parts]
    w_own, w_sib, quads, hot = refs[n_parts : n_parts + 4]
    pos = n_parts + 4
    acc_in = refs[pos] if has_acc else None
    out, acc, qacc = refs[pos + has_acc :]
    j = pl.program_id(0)

    @pl.when(j == 0)
    def _():
        acc[...] = jnp.zeros_like(acc)
        qacc[...] = jnp.zeros_like(qacc)

    rows = w_own.shape[1]
    own, sib, quad = None, None, None
    for i in range(wide):
        cols = slice(i * KB, (i + 1) * KB)
        pieces = [r[:, cols].astype(F32) for r in parts]
        used = sum(p.shape[0] for p in pieces)
        pieces.append(jnp.zeros((LANES - used, KB), F32))
        p32 = jnp.concatenate(pieces, axis=0)
        pb = p32.astype(BF16)
        d_own = lax.dot_general(w_own[i], pb, NT, preferred_element_type=F32)
        d_sib = lax.dot_general(w_sib[i], pb, NT, preferred_element_type=F32)
        sq = p32 * p32
        hi = sq.astype(BF16)
        lo = (sq - hi.astype(F32)).astype(BF16)
        hh = quads[:, cols]
        d_quad = lax.dot_general(hh, hi, NT, preferred_element_type=F32) + lax.dot_general(
            hh, lo, NT, preferred_element_type=F32
        )
        own = d_own if own is None else own + d_own
        sib = d_sib if sib is None else sib + d_sib
        quad = d_quad if quad is None else quad + d_quad
    acc[:rows, :] += own
    acc[rows:, :] += sib
    qacc[...] += quad

    @pl.when(j == nb - 1)
    def _():
        n_cls = qacc.shape[0] // 2
        q = qacc[:n_cls, :] + qacc[n_cls:, :]
        total = acc[...] - jnp.dot(hot[...], q, precision=PRECISE, preferred_element_type=F32)
        turned = jnp.transpose(total)[:used, :]
        if has_acc:
            turned = turned + acc_in[...]
        out[...] = turned


def score(parts, w_own, w_sib, quads, hot, quarter, acc_in):
    part_rows = parts[0].shape[0]
    rows = w_own.shape[1]
    wide = 2
    kb = wide * KB
    nb = w_own.shape[0] // wide
    used = part_rows * len(parts)
    off = quarter * nb
    in_specs = [pl.BlockSpec((part_rows, kb), lambda j: (0, j)) for _ in parts]
    in_specs += [
        pl.BlockSpec((wide, rows, KB), lambda j: (j, 0, 0)),
        pl.BlockSpec((wide, rows, KB), lambda j: (j, 0, 0)),
        pl.BlockSpec((quads.shape[0], kb), lambda j: (0, off + j)),
        full(hot.shape),
    ]
    args = [*parts, w_own, w_sib, quads, hot]
    if acc_in is not None:
        in_specs.append(full((used, 2 * rows)))
        args.append(acc_in)
    return pl.pallas_call(
        functools.partial(score_kernel, len(parts), acc_in is not None, nb, wide),
        grid=(nb,),
        in_specs=in_specs,
        out_specs=full((used, 2 * rows)),
        out_shape=jax.ShapeDtypeStruct((used, 2 * rows), F32),
        scratch_shapes=[
            pltpu.VMEM((2 * rows, LANES), F32),
            pltpu.VMEM((quads.shape[0], LANES), F32),
        ],
        compiler_params=params(),
        cost_estimate=CHEAP,
        name="score",
    )(*args)


def stat_kernel(mine, recv, cnt, out, st_out):
    rows = mine.shape[1] // 2
    r = recv[...]
    total = mine[...] + jnp.concatenate([r[:, rows:], r[:, :rows]], axis=1)
    out[...] = total
    peak = jnp.max(total, axis=0, keepdims=True)
    st_out[0:1, :] = peak
    st_out[1:2, :] = jnp.sum(jnp.exp(total - peak) * cnt[...], axis=0, keepdims=True)


def merge(stats):
    peak = stats[0][0:1, :]
    for s in stats[1:]:
        peak = jnp.maximum(peak, s[0:1, :])
    mass = jnp.zeros_like(peak)
    for s in stats:
        mass = mass + s[1:2, :] * jnp.exp(s[0:1, :] - peak)
    return peak, mass


def merge_kernel(*refs):
    peak, mass = merge(refs[:-1])
    refs[-1][0:1, :] = peak
    refs[-1][1:2, :] = mass


def chance_kernel(n, *refs):
    scores, cnt, hot = refs[:3]
    p_out, t_out, l_out = refs[3 + n :]
    peak, mass = merge(refs[3 : 3 + n])
    shift = peak + jnp.log(mass)
    own = l_out.shape[1]
    lw = scores[...] - shift
    l_out[...] = lw[:, :own]
    chance = jnp.exp(lw).astype(BF16).astype(F32)
    per = (chance * cnt[...]).astype(BF16)
    p_out[...] = per
    tot = jnp.dot(per, hot[...], preferred_element_type=F32)
    hi = tot.astype(BF16).astype(F32)
    t_out[...] = hi + pltpu.roll(tot - hi, 32, 1)


def whole(kernel, out_shape, name, *args):
    return pl.pallas_call(
        kernel,
        out_shape=out_shape,
        compiler_params=pltpu.CompilerParams(vmem_limit_bytes=VMEM_LIMIT),
        cost_estimate=CHEAP,
        name=name,
    )(*args)


def back_kernel(n_parts, nb, wide, tail, *refs):
    per, w_own, w_sib, tot = refs[:4]
    outs = refs[4:]
    j = pl.program_id(0)
    rows = w_own.shape[1]
    h = per.shape[0] // n_parts
    for i in range(wide):
        res = lax.dot_general(
            per[:, :rows], w_own[i], NN, preferred_element_type=F32
        ) + lax.dot_general(per[:, rows:], w_sib[i], NN, preferred_element_type=F32)
        at = pl.ds(pl.multiple_of(j * wide * KB + i * KB, KB), KB)
        for k, o in enumerate(outs):
            o[:, at] = res[k * h : (k + 1) * h, :].astype(BF16)
    if tail:

        @pl.when(j == nb - 1)
        def _():
            for k, o in enumerate(outs):
                o[:, nb * wide * KB :] = tot[k * h : (k + 1) * h, :].astype(BF16)


def back(per, w_own, w_sib, tot, quarter, n_parts):
    blocks, rows, _ = w_own.shape
    wide = 2
    nb = blocks // wide
    h = per.shape[0] // n_parts
    tail = quarter == 0
    width = nb * wide * KB + (TAIL if tail else 0)
    return pl.pallas_call(
        functools.partial(back_kernel, n_parts, nb, wide, tail),
        grid=(nb,),
        in_specs=[
            full(per.shape),
            pl.BlockSpec((wide, rows, KB), lambda j: (j, 0, 0)),
            pl.BlockSpec((wide, rows, KB), lambda j: (j, 0, 0)),
            full(tot.shape),
        ],
        out_specs=[full((h, width))] * n_parts,
        out_shape=[jax.ShapeDtypeStruct((h, width), BF16)] * n_parts,
        compiler_params=params(),
        cost_estimate=CHEAP,
        name="back",
    )(per, w_own, w_sib, tot)


def add_tail(tail):
    tot = tail + pltpu.roll(tail, TAIL - 32, 1)
    lane = lax.broadcasted_iota(jnp.int32, tail.shape, 1)
    tot = jnp.where(lane < 32, tot, 0.0)
    hi = tot.astype(BF16).astype(F32)
    return hi + pltpu.roll(tot - hi, 32, 1)


def add_kernel(n, tail, *refs):
    out = refs[n]
    width = out.shape[1] - (TAIL if tail else 0)
    total = refs[0][...].astype(F32)
    for r in refs[1:n]:
        total = total + r[...].astype(F32)
    if tail:
        out[:, :width] = total[:, :width].astype(BF16)
        out[:, width:] = add_tail(total[:, width:]).astype(BF16)
    else:
        out[...] = total.astype(BF16)


def add(*arrays, tail):
    return whole(
        functools.partial(add_kernel, len(arrays), tail),
        jax.ShapeDtypeStruct(arrays[0].shape, BF16),
        "add",
        *arrays,
    )


def tie(value, *others):
    return lax.optimization_barrier((value, *others))[0]


def shards(images, classes, contrast, noise_weight, projections, proj_index):
    half = contrast.shape[1]
    quart = half // 2
    n_cls = contrast.shape[0]
    own_rows = projections.shape[1]
    h = 2 * own_rows
    me = lax.axis_index("img")
    core = (me % NC).astype(jnp.int32)
    chip = (me // NC).astype(jnp.int32)
    first = core == 0
    noise = noise_weight[None, :]

    mine = projections[0]
    low, high = mine[:, :half], mine[:, half:]
    got = to_core(jnp.where(first, high, low))
    kept = jnp.where(first, low, high)
    shard = jnp.where(
        first, jnp.concatenate([kept, got], axis=0), jnp.concatenate([got, kept], axis=0)
    )
    own_a, own_b = shard[:, :quart], shard[:, quart:]
    xm_a, xp_a, zz = to_xp(own_a), to_xm(own_a), to_z(shard)
    xm_b, xp_b = to_xp(own_b), to_xm(own_b)
    zz_a, zz_b = zz[:, :quart], zz[:, quart:]
    x2_a, x2_b = to_xp(xm_a), to_xm(xp_b)
    fz_a, fz_b = tie(zz_a, x2_a, x2_b), tie(zz_b, x2_a, x2_b)
    zm_a, zp_a, z2_a = to_xp(fz_a), to_xm(fz_a), to_z(x2_a)
    zm_b, zp_b, z2_b = to_xp(fz_b), to_xm(fz_b), to_z(x2_b)

    sib_classes = to_core(classes)
    ids = jnp.arange(n_cls, dtype=jnp.int32)[None, :]
    hot_own = (classes[:, None] == ids).astype(BF16)
    both_classes = jnp.concatenate([classes, sib_classes])
    hot = (both_classes[:, None] == ids).astype(F32)
    hot_wide = (both_classes[:, None] == jnp.arange(TAIL, dtype=jnp.int32)[None, :]).astype(BF16)
    hot3 = jnp.concatenate([hot_own] * 3, axis=1)
    w_own, w_sib = [], []
    for quarter in range(2):
        before = (xm_b, xp_b) if quarter else (shard,)
        after = (x2_a, x2_b) if quarter else (xm_b, xp_b, zz)
        at = tie(core.reshape(1), *before)
        keep, give = weigh(at, images, hot3, contrast, noise, quarter)
        w_own.append(keep)
        w_sib.append(to_core(tie(give, *after)))
    quads = quad_table(contrast, noise)

    target = proj_index // h
    dz = (target // NX) ^ (chip // NX)
    dx = (target - chip) % NX
    near = jnp.where(dx == 0, 0, jnp.where(dx == 1, 1, jnp.where(dx == 3, 2, 4)))
    far = jnp.where(dx == 0, 3, jnp.where(dx == 1, 5, jnp.where(dx == 3, 6, 7)))
    rel = jnp.where(dz == 0, near, far) * h + proj_index % h
    block_width = 8 * h
    choose = (jnp.arange(block_width, dtype=jnp.int32)[:, None] == rel[None, :]).astype(F32)
    counts = jnp.sum(choose, axis=1, keepdims=True)

    table = (quads, hot)
    part = [own_a, xp_a, xm_a, zz_a, x2_a, zp_a, zm_a, z2_a]
    mine = score(part, w_own[0], w_sib[0], *table, 0, None)
    part = [own_b, xp_b, xm_b, zz_b, x2_b, zp_b, zm_b, z2_b]
    mine = score(part, w_own[1], w_sib[1], *table, 1, mine)
    stat_shape = jax.ShapeDtypeStruct((2, mine.shape[1]), F32)
    scores, stat = whole(
        stat_kernel,
        [jax.ShapeDtypeStruct(mine.shape, F32), stat_shape],
        "stat",
        mine,
        to_core(mine),
        counts,
    )
    stat = whole(
        merge_kernel,
        stat_shape,
        "merge",
        stat,
        lax.ppermute(stat, "ori", ori_perm(1, 0)),
    )
    stats = [stat] + [lax.ppermute(stat, "ori", ori_perm(0, y)) for y in range(1, 4)]
    per, tot, local = whole(
        functools.partial(chance_kernel, len(stats)),
        [
            jax.ShapeDtypeStruct((block_width, stat.shape[1]), BF16),
            jax.ShapeDtypeStruct((block_width, TAIL), F32),
            jax.ShapeDtypeStruct((block_width, stat.shape[1] // 2), F32),
        ],
        "chance",
        scores,
        counts,
        hot_wide,
        *stats,
    )
    log_weights = lax.dot_general(
        local, choose, (((0,), (0,)), ((), ())), precision=PRECISE
    )

    bo_a, bxp_a, bxm_a, bzz_a, bx2_a, bzp_a, bzm_a, bz2_a = back(
        per, w_own[0], w_sib[0], tot, 0, 8
    )
    bo_b, bxp_b, bxm_b, bzz_b, bx2_b, bzp_b, bzm_b, bz2_b = back(
        per, w_own[1], w_sib[1], tot, 1, 8
    )
    r_z2a, r_zma, r_zpa = to_z(bz2_a), to_xm(bzm_a), to_xp(bzp_a)
    r_z2b, r_zmb = to_z(bz2_b), to_xm(bzm_b)
    r_zpb = to_xp(tie(bzp_b, r_z2a))
    r_x2a = to_xm(tie(add(bx2_a, r_z2a, tail=True), r_zma))
    r_x2b = to_xp(tie(add(bx2_b, r_z2b, tail=False), r_zpa))
    r_zza = to_z(add(bzz_a, r_zma, r_zpa, tail=True))
    r_zzb = to_z(add(bzz_b, r_zmb, r_zpb, tail=False))
    r_xmb, r_xpa = to_xm(tie(bxm_b, r_zmb)), to_xp(tie(bxp_a, r_zpb))
    r_xma = to_xm(add(bxm_a, r_x2a, tail=True))
    r_xpb = to_xp(add(bxp_b, r_x2b, tail=False))
    fin_a = add(bo_a, r_xpa, r_xma, r_zza, tail=True)
    fin_b = add(bo_b, r_xpb, r_xmb, r_zzb, tail=False)

    fin = jnp.concatenate([fin_a[:, :quart], fin_b], axis=1)
    got = to_core(jnp.where(first, fin[own_rows:], fin[:own_rows]))
    kept = jnp.where(first, fin[:own_rows], fin[own_rows:])
    back_sums = jnp.where(
        first, jnp.concatenate([kept, got], axis=1), jnp.concatenate([got, kept], axis=1)
    )
    ends = fin_a[:, quart:].astype(F32)
    totals = ends[:, :n_cls] + ends[:, n_cls : 2 * n_cls]
    totals = jnp.where(first, totals[:own_rows], totals[own_rows:])
    contrast_mass = jnp.dot(totals, contrast * contrast, precision=PRECISE)
    return log_weights, back_sums[None], contrast_mass[None]


def solution(mesh):
    in_specs = (P("img", None), P("img"), P(), P(), P("ori", "img", None), P("ori"))
    out_specs = (P("img", "ori"), P("ori", "img", None), P("ori", "img", None))
    return jax.shard_map(shards, mesh=mesh, in_specs=in_specs, out_specs=out_specs, check_vma=False)
```

```python
import functools

import jax
import jax.numpy as jnp
from jax import lax
from jax.experimental import pallas as pl
from jax.experimental.pallas import tpu as pltpu
from jax.sharding import PartitionSpec as P

PRECISE = lax.Precision.HIGHEST
F32 = jnp.float32
BF16 = jnp.bfloat16
NX, NC = 4, 2
TAIL = 128
LANES = 256
KB = 1024
CHEAP = pl.CostEstimate(flops=1024, bytes_accessed=1024, transcendentals=0)
NT = (((1,), (1,)), ((), ()))
NN = (((1,), (0,)), ((), ()))
VMEM_LIMIT = 48 * 1024 * 1024


def img_perm(dz, dx, dc):
    pairs = []
    for z in range(2):
        for x in range(NX):
            for c in range(NC):
                src = (z * NX + x) * NC + c
                dst = ((z ^ dz) * NX + (x + dx) % NX) * NC + (c ^ dc)
                pairs.append((src, dst))
    return pairs


def ori_perm(dz, dy):
    return [(z * 4 + y, (z ^ dz) * 4 + (y + dy) % 4) for z in range(2) for y in range(4)]


def to_xp(v):
    return lax.ppermute(v, "img", img_perm(0, 1, 0))


def to_xm(v):
    return lax.ppermute(v, "img", img_perm(0, -1, 0))


def to_z(v):
    return lax.ppermute(v, "img", img_perm(1, 0, 0))


def to_core(v):
    return lax.ppermute(v, "img", img_perm(0, 0, 1))


def params(mib=48):
    return pltpu.CompilerParams(
        dimension_semantics=("arbitrary",), vmem_limit_bytes=mib * 1024 * 1024
    )


def full(shape):
    return pl.BlockSpec(shape, lambda j: (0,) * len(shape))


def weigh_kernel(core, keep, give, hot3, contrast, noise, keep_out, give_out):
    amp = contrast[...] * noise[...]
    a1 = amp.astype(BF16)
    rest = amp - a1.astype(F32)
    a2 = rest.astype(BF16)
    a3 = (rest - a2.astype(F32)).astype(BF16)
    table = jnp.concatenate([a1, a2, a3], axis=0)
    amplitude = lax.dot_general(hot3[...], table, NN, preferred_element_type=F32)
    for img, out in ((give, give_out), (keep, keep_out)):
        value = (img[...].astype(F32) * amplitude).astype(BF16)
        for i in range(out.shape[0]):
            out[i] = value[:, i * KB : (i + 1) * KB]


def weigh(core, images, hot3, contrast, noise):
    rows, cols = images.shape
    half = cols // 2
    wide = 4
    kb = wide * KB
    nb = half // kb
    n_cls = contrast.shape[0]
    return pl.pallas_call(
        weigh_kernel,
        grid_spec=pltpu.PrefetchScalarGridSpec(
            num_scalar_prefetch=1,
            grid=(nb,),
            in_specs=[
                pl.BlockSpec((rows, kb), lambda j, s: (0, s[0] * nb + j)),
                pl.BlockSpec((rows, kb), lambda j, s: (0, (1 - s[0]) * nb + j)),
                pl.BlockSpec(hot3.shape, lambda j, s: (0, 0)),
                pl.BlockSpec((n_cls, kb), lambda j, s: (0, j)),
                pl.BlockSpec((1, kb), lambda j, s: (0, j)),
            ],
            out_specs=[pl.BlockSpec((wide, rows, KB), lambda j, s: (j, 0, 0))] * 2,
        ),
        out_shape=[jax.ShapeDtypeStruct((half // KB, rows, KB), BF16)] * 2,
        compiler_params=params(),
        cost_estimate=CHEAP,
        name="weigh",
    )(core, images, images, hot3, contrast, noise)


def table_kernel(contrast, noise, out):
    hq = 0.5 * contrast[...] * contrast[...] * noise[...]
    h1 = hq.astype(BF16)
    h2 = (hq - h1.astype(F32)).astype(BF16)
    out[...] = jnp.concatenate([h1, h2], axis=0)


def quad_table(contrast, noise):
    n_cls, half = contrast.shape
    kb = 4 * KB
    return pl.pallas_call(
        table_kernel,
        grid=(half // kb,),
        in_specs=[
            pl.BlockSpec((n_cls, kb), lambda j: (0, j)),
            pl.BlockSpec((1, kb), lambda j: (0, j)),
        ],
        out_specs=pl.BlockSpec((2 * n_cls, kb), lambda j: (0, j)),
        out_shape=jax.ShapeDtypeStruct((2 * n_cls, half), BF16),
        compiler_params=params(),
        cost_estimate=CHEAP,
        name="table",
    )(contrast, noise)


def score_kernel(n_parts, has_acc, nb, wide, *refs):
    parts = refs[:n_parts]
    w_own, w_sib, quads, hot = refs[n_parts : n_parts + 4]
    pos = n_parts + 4
    acc_in = refs[pos] if has_acc else None
    out, acc, qacc = refs[pos + has_acc :]
    j = pl.program_id(0)

    @pl.when(j == 0)
    def _():
        acc[...] = jnp.zeros_like(acc)
        qacc[...] = jnp.zeros_like(qacc)

    rows = w_own.shape[1]
    own, sib, quad = None, None, None
    for i in range(wide):
        cols = slice(i * KB, (i + 1) * KB)
        pieces = [r[:, cols].astype(F32) for r in parts]
        used = sum(p.shape[0] for p in pieces)
        pieces.append(jnp.zeros((LANES - used, KB), F32))
        p32 = jnp.concatenate(pieces, axis=0)
        pb = p32.astype(BF16)
        d_own = lax.dot_general(w_own[i], pb, NT, preferred_element_type=F32)
        d_sib = lax.dot_general(w_sib[i], pb, NT, preferred_element_type=F32)
        sq = p32 * p32
        hi = sq.astype(BF16)
        lo = (sq - hi.astype(F32)).astype(BF16)
        hh = quads[:, cols]
        d_quad = lax.dot_general(hh, hi, NT, preferred_element_type=F32) + lax.dot_general(
            hh, lo, NT, preferred_element_type=F32
        )
        own = d_own if own is None else own + d_own
        sib = d_sib if sib is None else sib + d_sib
        quad = d_quad if quad is None else quad + d_quad
    acc[:rows, :] += own
    acc[rows:, :] += sib
    qacc[...] += quad

    @pl.when(j == nb - 1)
    def _():
        n_cls = qacc.shape[0] // 2
        q = qacc[:n_cls, :] + qacc[n_cls:, :]
        total = acc[...] - jnp.dot(hot[...], q, precision=PRECISE, preferred_element_type=F32)
        turned = jnp.transpose(total)[:used, :]
        if has_acc:
            turned = turned + acc_in[...]
        out[...] = turned


def score(parts, w_own, w_sib, quads, hot, quarter, acc_in):
    part_rows = parts[0].shape[0]
    rows = w_own.shape[1]
    wide = 4
    kb = wide * KB
    nb = w_own.shape[0] // wide // 2
    used = part_rows * len(parts)
    off = quarter * nb
    in_specs = []
    for p in parts:
        at = off if p.shape[1] > nb * kb else 0
        in_specs.append(pl.BlockSpec((part_rows, kb), lambda j, at=at: (0, at + j)))
    in_specs += [
        pl.BlockSpec((wide, rows, KB), lambda j: (off + j, 0, 0)),
        pl.BlockSpec((wide, rows, KB), lambda j: (off + j, 0, 0)),
        pl.BlockSpec((quads.shape[0], kb), lambda j: (0, off + j)),
        full(hot.shape),
    ]
    args = [*parts, w_own, w_sib, quads, hot]
    if acc_in is not None:
        in_specs.append(full((used, 2 * rows)))
        args.append(acc_in)
    return pl.pallas_call(
        functools.partial(score_kernel, len(parts), acc_in is not None, nb, wide),
        grid=(nb,),
        in_specs=in_specs,
        out_specs=full((used, 2 * rows)),
        out_shape=jax.ShapeDtypeStruct((used, 2 * rows), F32),
        scratch_shapes=[
            pltpu.VMEM((2 * rows, LANES), F32),
            pltpu.VMEM((quads.shape[0], LANES), F32),
        ],
        compiler_params=params(),
        cost_estimate=CHEAP,
        name="score",
    )(*args)


def stat_kernel(mine, recv, cnt, out, st_out):
    rows = mine.shape[1] // 2
    r = recv[...]
    total = mine[...] + jnp.concatenate([r[:, rows:], r[:, :rows]], axis=1)
    out[...] = total
    peak = jnp.max(total, axis=0, keepdims=True)
    st_out[0:1, :] = peak
    st_out[1:2, :] = jnp.sum(jnp.exp(total - peak) * cnt[...], axis=0, keepdims=True)


def merge(stats):
    peak = stats[0][0:1, :]
    for s in stats[1:]:
        peak = jnp.maximum(peak, s[0:1, :])
    mass = jnp.zeros_like(peak)
    for s in stats:
        mass = mass + s[1:2, :] * jnp.exp(s[0:1, :] - peak)
    return peak, mass


def merge_kernel(*refs):
    peak, mass = merge(refs[:-1])
    refs[-1][0:1, :] = peak
    refs[-1][1:2, :] = mass


def chance_kernel(n, *refs):
    scores, cnt, hot = refs[:3]
    p_out, t_out, l_out = refs[3 + n :]
    peak, mass = merge(refs[3 : 3 + n])
    shift = peak + jnp.log(mass)
    own = l_out.shape[1]
    lw = scores[...] - shift
    l_out[...] = lw[:, :own]
    chance = jnp.exp(lw).astype(BF16).astype(F32)
    per = (chance * cnt[...]).astype(BF16)
    p_out[...] = per
    tot = jnp.dot(per, hot[...], preferred_element_type=F32)
    hi = tot.astype(BF16).astype(F32)
    t_out[...] = hi + pltpu.roll(tot - hi, 32, 1)


def whole(kernel, out_shape, name, *args):
    return pl.pallas_call(
        kernel,
        out_shape=out_shape,
        compiler_params=pltpu.CompilerParams(vmem_limit_bytes=VMEM_LIMIT),
        cost_estimate=CHEAP,
        name=name,
    )(*args)


def back_kernel(n_parts, nb, wide, tail, *refs):
    per, w_own, w_sib, tot = refs[:4]
    outs = refs[4:]
    j = pl.program_id(0)
    rows = w_own.shape[1]
    h = per.shape[0] // n_parts
    for i in range(wide):
        res = lax.dot_general(
            per[:, :rows], w_own[i], NN, preferred_element_type=F32
        ) + lax.dot_general(per[:, rows:], w_sib[i], NN, preferred_element_type=F32)
        at = pl.ds(pl.multiple_of(j * wide * KB + i * KB, KB), KB)
        for k, o in enumerate(outs):
            o[:, at] = res[k * h : (k + 1) * h, :].astype(BF16)
    if tail:

        @pl.when(j == nb - 1)
        def _():
            for k, o in enumerate(outs):
                o[:, nb * wide * KB :] = tot[k * h : (k + 1) * h, :].astype(BF16)


def back(per, w_own, w_sib, tot, quarter, n_parts):
    blocks, rows, _ = w_own.shape
    wide = 4
    nb = blocks // wide // 2
    off = quarter * nb
    h = per.shape[0] // n_parts
    tail = quarter == 0
    width = nb * wide * KB + (TAIL if tail else 0)
    return pl.pallas_call(
        functools.partial(back_kernel, n_parts, nb, wide, tail),
        grid=(nb,),
        in_specs=[
            full(per.shape),
            pl.BlockSpec((wide, rows, KB), lambda j: (off + j, 0, 0)),
            pl.BlockSpec((wide, rows, KB), lambda j: (off + j, 0, 0)),
            full(tot.shape),
        ],
        out_specs=[full((h, width))] * n_parts,
        out_shape=[jax.ShapeDtypeStruct((h, width), BF16)] * n_parts,
        compiler_params=params(),
        cost_estimate=CHEAP,
        name="back",
    )(per, w_own, w_sib, tot)


def add_tail(tail):
    tot = tail + pltpu.roll(tail, TAIL - 32, 1)
    lane = lax.broadcasted_iota(jnp.int32, tail.shape, 1)
    tot = jnp.where(lane < 32, tot, 0.0)
    hi = tot.astype(BF16).astype(F32)
    return hi + pltpu.roll(tot - hi, 32, 1)


def add_kernel(n, tail, *refs):
    out = refs[n]
    width = out.shape[1] - (TAIL if tail else 0)
    total = refs[0][...].astype(F32)
    for r in refs[1:n]:
        total = total + r[...].astype(F32)
    if tail:
        out[:, :width] = total[:, :width].astype(BF16)
        out[:, width:] = add_tail(total[:, width:]).astype(BF16)
    else:
        out[...] = total.astype(BF16)


def add(*arrays, tail):
    return whole(
        functools.partial(add_kernel, len(arrays), tail),
        jax.ShapeDtypeStruct(arrays[0].shape, BF16),
        "add",
        *arrays,
    )


def tie(value, *others):
    return lax.optimization_barrier((value, *others))[0]


def shards(images, classes, contrast, noise_weight, projections, proj_index):
    half = contrast.shape[1]
    quart = half // 2
    n_cls = contrast.shape[0]
    own_rows = projections.shape[1]
    h = 2 * own_rows
    me = lax.axis_index("img")
    core = (me % NC).astype(jnp.int32)
    chip = (me // NC).astype(jnp.int32)
    first = core == 0
    noise = noise_weight[None, :]

    mine = projections[0]
    low, high = mine[:, :half], mine[:, half:]
    got = to_core(jnp.where(first, high, low))
    kept = jnp.where(first, low, high)
    own_a, own_b = (
        jnp.where(
            first,
            jnp.concatenate([kept[:, cols], got[:, cols]], axis=0),
            jnp.concatenate([got[:, cols], kept[:, cols]], axis=0),
        )
        for cols in (slice(0, quart), slice(quart, half))
    )
    xm_a, xp_b, zz_a = to_xp(own_a), to_xm(own_b), to_z(own_a)
    xm_b, xp_a = to_xp(own_b), to_xm(own_a)
    x2_a, x2_b = to_xp(xm_a), to_xm(xp_b)
    zz_b = to_z(tie(own_b, zz_a))
    fz_a, fz_b = tie(zz_a, x2_a, x2_b), tie(zz_b, x2_a, x2_b)
    zm_a, zp_a, z2_a = to_xp(fz_a), to_xm(fz_a), to_z(x2_a)

    sib_classes = to_core(classes)
    ids = jnp.arange(n_cls, dtype=jnp.int32)[None, :]
    hot_own = (classes[:, None] == ids).astype(BF16)
    both_classes = jnp.concatenate([classes, sib_classes])
    hot = (both_classes[:, None] == ids).astype(F32)
    hot_wide = (both_classes[:, None] == jnp.arange(TAIL, dtype=jnp.int32)[None, :]).astype(BF16)
    hot3 = jnp.concatenate([hot_own] * 3, axis=1)
    w_own, give = weigh(tie(core.reshape(1), own_a, sib_classes), images, hot3, contrast, noise)
    w_sib = to_core(tie(give, xm_a, xm_b, xp_a, xp_b, zz_a))
    quads = quad_table(tie(contrast, xm_a), noise)
    zm_b, zp_b, z2_b = to_xp(tie(fz_b, quads)), to_xm(tie(fz_b, w_sib)), to_z(tie(x2_b, z2_a))

    target = proj_index // h
    dz = (target // NX) ^ (chip // NX)
    dx = (target - chip) % NX
    near = jnp.where(dx == 0, 0, jnp.where(dx == 1, 1, jnp.where(dx == 3, 2, 4)))
    far = jnp.where(dx == 0, 3, jnp.where(dx == 1, 5, jnp.where(dx == 3, 6, 7)))
    rel = jnp.where(dz == 0, near, far) * h + proj_index % h
    block_width = 8 * h
    choose = (jnp.arange(block_width, dtype=jnp.int32)[:, None] == rel[None, :]).astype(F32)
    counts = jnp.sum(choose, axis=1, keepdims=True)

    table = (quads, hot)
    part = [own_a, xp_a, xm_a, zz_a, x2_a, zp_a, zm_a, z2_a]
    mine = score(part, w_own, w_sib, *table, 0, None)
    part = [own_b, xp_b, xm_b, zz_b, x2_b, zp_b, zm_b, z2_b]
    mine = score(part, w_own, w_sib, *table, 1, mine)
    stat_shape = jax.ShapeDtypeStruct((2, mine.shape[1]), F32)
    scores, stat = whole(
        stat_kernel,
        [jax.ShapeDtypeStruct(mine.shape, F32), stat_shape],
        "stat",
        mine,
        to_core(mine),
        counts,
    )
    stat = whole(
        merge_kernel,
        stat_shape,
        "merge",
        stat,
        lax.ppermute(stat, "ori", ori_perm(1, 0)),
    )
    stats = [stat] + [lax.ppermute(stat, "ori", ori_perm(0, y)) for y in range(1, 4)]
    per, tot, local = whole(
        functools.partial(chance_kernel, len(stats)),
        [
            jax.ShapeDtypeStruct((block_width, stat.shape[1]), BF16),
            jax.ShapeDtypeStruct((block_width, TAIL), F32),
            jax.ShapeDtypeStruct((block_width, stat.shape[1] // 2), F32),
        ],
        "chance",
        scores,
        counts,
        hot_wide,
        *stats,
    )
    log_weights = lax.dot_general(
        local, choose, (((0,), (0,)), ((), ())), precision=PRECISE
    )

    bo_a, bxp_a, bxm_a, bzz_a, bx2_a, bzp_a, bzm_a, bz2_a = back(
        per, w_own, w_sib, tot, 0, 8
    )
    bo_b, bxp_b, bxm_b, bzz_b, bx2_b, bzp_b, bzm_b, bz2_b = back(
        per, w_own, w_sib, tot, 1, 8
    )
    r_z2a, r_zma, r_zpa = to_z(bz2_a), to_xm(bzm_a), to_xp(bzp_a)
    r_z2b, r_zmb = to_z(bz2_b), to_xm(bzm_b)
    r_zpb = to_xp(tie(bzp_b, r_z2a))
    r_x2a = to_xm(tie(add(bx2_a, r_z2a, tail=True), r_zma))
    r_x2b = to_xp(tie(add(bx2_b, r_z2b, tail=False), r_zpa))
    r_zza = to_z(add(bzz_a, r_zma, r_zpa, tail=True))
    r_zzb = to_z(add(bzz_b, r_zmb, r_zpb, tail=False))
    r_xmb, r_xpa = to_xm(tie(bxm_b, r_zmb)), to_xp(tie(bxp_a, r_zpb))
    r_xma = to_xm(add(bxm_a, r_x2a, tail=True))
    r_xpb = to_xp(add(bxp_b, r_x2b, tail=False))
    fin_a = add(bo_a, r_xpa, r_xma, r_zza, tail=True)
    fin_b = add(bo_b, r_xpb, r_xmb, r_zzb, tail=False)

    fin = jnp.concatenate([fin_a[:, :quart], fin_b], axis=1)
    got = to_core(jnp.where(first, fin[own_rows:], fin[:own_rows]))
    kept = jnp.where(first, fin[:own_rows], fin[own_rows:])
    back_sums = jnp.where(
        first, jnp.concatenate([kept, got], axis=1), jnp.concatenate([got, kept], axis=1)
    )
    ends = fin_a[:, quart:].astype(F32)
    totals = ends[:, :n_cls] + ends[:, n_cls : 2 * n_cls]
    totals = jnp.where(first, totals[:own_rows], totals[own_rows:])
    contrast_mass = jnp.dot(totals, contrast * contrast, precision=PRECISE)
    return log_weights, back_sums[None], contrast_mass[None]


def solution(mesh):
    in_specs = (P("img", None), P("img"), P(), P(), P("ori", "img", None), P("ori"))
    out_specs = (P("img", "ori"), P("ori", "img", None), P("ori", "img", None))
    return jax.shard_map(shards, mesh=mesh, in_specs=in_specs, out_specs=out_specs, check_vma=False)
```

```python
import functools

import jax
import jax.numpy as jnp
from jax import lax
from jax.experimental import pallas as pl
from jax.experimental.pallas import tpu as pltpu
from jax.sharding import PartitionSpec as P

PRECISE = lax.Precision.HIGHEST
F32 = jnp.float32
BF16 = jnp.bfloat16
NX, NC = 4, 2
TAIL = 128
LANES = 256
KB = 1024
CHEAP = pl.CostEstimate(flops=1024, bytes_accessed=1024, transcendentals=0)
NT = (((1,), (1,)), ((), ()))
NN = (((1,), (0,)), ((), ()))
VMEM_LIMIT = 48 * 1024 * 1024


def img_perm(dz, dx, dc):
    pairs = []
    for z in range(2):
        for x in range(NX):
            for c in range(NC):
                src = (z * NX + x) * NC + c
                dst = ((z ^ dz) * NX + (x + dx) % NX) * NC + (c ^ dc)
                pairs.append((src, dst))
    return pairs


def ori_perm(dz, dy):
    return [(z * 4 + y, (z ^ dz) * 4 + (y + dy) % 4) for z in range(2) for y in range(4)]


def to_xp(v):
    return lax.ppermute(v, "img", img_perm(0, 1, 0))


def to_xm(v):
    return lax.ppermute(v, "img", img_perm(0, -1, 0))


def to_z(v):
    return lax.ppermute(v, "img", img_perm(1, 0, 0))


def to_core(v):
    return lax.ppermute(v, "img", img_perm(0, 0, 1))


def params(mib=48):
    return pltpu.CompilerParams(
        dimension_semantics=("arbitrary",), vmem_limit_bytes=mib * 1024 * 1024
    )


def full(shape):
    return pl.BlockSpec(shape, lambda j: (0,) * len(shape))


def weigh_kernel(core, keep, give, hot3, contrast, noise, keep_out, give_out, quad_out):
    amp = contrast[...] * noise[...]
    hq = 0.5 * contrast[...] * amp
    h1 = hq.astype(BF16)
    h2 = (hq - h1.astype(F32)).astype(BF16)
    quad_out[...] = jnp.concatenate([h1, h2], axis=0)
    a1 = amp.astype(BF16)
    rest = amp - a1.astype(F32)
    a2 = rest.astype(BF16)
    a3 = (rest - a2.astype(F32)).astype(BF16)
    table = jnp.concatenate([a1, a2, a3], axis=0)
    amplitude = lax.dot_general(hot3[...], table, NN, preferred_element_type=F32)
    for img, out in ((give, give_out), (keep, keep_out)):
        value = (img[...].astype(F32) * amplitude).astype(BF16)
        for i in range(out.shape[0]):
            out[i] = value[:, i * KB : (i + 1) * KB]


def weigh(core, images, hot3, contrast, noise):
    rows, cols = images.shape
    half = cols // 2
    wide = 4
    kb = wide * KB
    nb = half // kb
    n_cls = contrast.shape[0]
    return pl.pallas_call(
        weigh_kernel,
        grid_spec=pltpu.PrefetchScalarGridSpec(
            num_scalar_prefetch=1,
            grid=(nb,),
            in_specs=[
                pl.BlockSpec((rows, kb), lambda j, s: (0, s[0] * nb + j)),
                pl.BlockSpec((rows, kb), lambda j, s: (0, (1 - s[0]) * nb + j)),
                pl.BlockSpec(hot3.shape, lambda j, s: (0, 0)),
                pl.BlockSpec((n_cls, kb), lambda j, s: (0, j)),
                pl.BlockSpec((1, kb), lambda j, s: (0, j)),
            ],
            out_specs=[
                pl.BlockSpec((wide, rows, KB), lambda j, s: (j, 0, 0)),
                pl.BlockSpec((wide, rows, KB), lambda j, s: (j, 0, 0)),
                pl.BlockSpec((2 * n_cls, kb), lambda j, s: (0, j)),
            ],
        ),
        out_shape=[
            jax.ShapeDtypeStruct((half // KB, rows, KB), BF16),
            jax.ShapeDtypeStruct((half // KB, rows, KB), BF16),
            jax.ShapeDtypeStruct((2 * n_cls, half), BF16),
        ],
        compiler_params=params(56),
        cost_estimate=CHEAP,
        name="weigh",
    )(core, images, images, hot3, contrast, noise)


def score_kernel(n_parts, has_acc, nb, wide, *refs):
    parts = refs[:n_parts]
    w_own, w_sib, quads, hot = refs[n_parts : n_parts + 4]
    pos = n_parts + 4
    acc_in = refs[pos] if has_acc else None
    out, acc, qacc = refs[pos + has_acc :]
    j = pl.program_id(0)

    @pl.when(j == 0)
    def _():
        acc[...] = jnp.zeros_like(acc)
        qacc[...] = jnp.zeros_like(qacc)

    rows = w_own.shape[1]
    own, sib, quad = None, None, None
    for i in range(wide):
        cols = slice(i * KB, (i + 1) * KB)
        pieces = [r[:, cols].astype(F32) for r in parts]
        used = sum(p.shape[0] for p in pieces)
        pieces.append(jnp.zeros((LANES - used, KB), F32))
        p32 = jnp.concatenate(pieces, axis=0)
        pb = p32.astype(BF16)
        d_own = lax.dot_general(w_own[i], pb, NT, preferred_element_type=F32)
        d_sib = lax.dot_general(w_sib[i], pb, NT, preferred_element_type=F32)
        sq = p32 * p32
        hi = sq.astype(BF16)
        lo = (sq - hi.astype(F32)).astype(BF16)
        hh = quads[:, cols]
        d_quad = lax.dot_general(hh, hi, NT, preferred_element_type=F32) + lax.dot_general(
            hh, lo, NT, preferred_element_type=F32
        )
        own = d_own if own is None else own + d_own
        sib = d_sib if sib is None else sib + d_sib
        quad = d_quad if quad is None else quad + d_quad
    acc[:rows, :] += own
    acc[rows:, :] += sib
    qacc[...] += quad

    @pl.when(j == nb - 1)
    def _():
        n_cls = qacc.shape[0] // 2
        q = qacc[:n_cls, :] + qacc[n_cls:, :]
        total = acc[...] - jnp.dot(hot[...], q, precision=PRECISE, preferred_element_type=F32)
        turned = jnp.transpose(total)[:used, :]
        if has_acc:
            turned = turned + acc_in[...]
        out[...] = turned


def score(parts, w_own, w_sib, quads, hot, quarter, acc_in):
    part_rows = parts[0].shape[0]
    rows = w_own.shape[1]
    wide = 4
    kb = wide * KB
    nb = w_own.shape[0] // wide // 2
    used = part_rows * len(parts)
    off = quarter * nb
    in_specs = []
    for p in parts:
        at = off if p.shape[1] > nb * kb else 0
        in_specs.append(pl.BlockSpec((part_rows, kb), lambda j, at=at: (0, at + j)))
    in_specs += [
        pl.BlockSpec((wide, rows, KB), lambda j: (off + j, 0, 0)),
        pl.BlockSpec((wide, rows, KB), lambda j: (off + j, 0, 0)),
        pl.BlockSpec((quads.shape[0], kb), lambda j: (0, off + j)),
        full(hot.shape),
    ]
    quads = pltpu.with_memory_space_constraint(quads, pltpu.HBM)
    args = [*parts, w_own, w_sib, quads, hot]
    if acc_in is not None:
        in_specs.append(full((used, 2 * rows)))
        args.append(acc_in)
    return pl.pallas_call(
        functools.partial(score_kernel, len(parts), acc_in is not None, nb, wide),
        grid=(nb,),
        in_specs=in_specs,
        out_specs=full((used, 2 * rows)),
        out_shape=jax.ShapeDtypeStruct((used, 2 * rows), F32),
        scratch_shapes=[
            pltpu.VMEM((2 * rows, LANES), F32),
            pltpu.VMEM((quads.shape[0], LANES), F32),
        ],
        compiler_params=params(),
        cost_estimate=CHEAP,
        name="score",
    )(*args)


def stat_kernel(mine, recv, cnt, out, st_out):
    rows = mine.shape[1] // 2
    r = recv[...]
    total = mine[...] + jnp.concatenate([r[:, rows:], r[:, :rows]], axis=1)
    out[...] = total
    peak = jnp.max(total, axis=0, keepdims=True)
    st_out[0:1, :] = peak
    st_out[1:2, :] = jnp.sum(jnp.exp(total - peak) * cnt[...], axis=0, keepdims=True)


def merge(stats):
    peak = stats[0][0:1, :]
    for s in stats[1:]:
        peak = jnp.maximum(peak, s[0:1, :])
    mass = jnp.zeros_like(peak)
    for s in stats:
        mass = mass + s[1:2, :] * jnp.exp(s[0:1, :] - peak)
    return peak, mass


def merge_kernel(*refs):
    peak, mass = merge(refs[:-1])
    refs[-1][0:1, :] = peak
    refs[-1][1:2, :] = mass


def chance_kernel(n, *refs):
    scores, cnt, hot = refs[:3]
    p_out, t_out, l_out = refs[3 + n :]
    peak, mass = merge(refs[3 : 3 + n])
    shift = peak + jnp.log(mass)
    own = l_out.shape[1]
    lw = scores[...] - shift
    l_out[...] = lw[:, :own]
    chance = jnp.exp(lw).astype(BF16).astype(F32)
    per = (chance * cnt[...]).astype(BF16)
    p_out[...] = per
    tot = jnp.dot(per, hot[...], preferred_element_type=F32)
    hi = tot.astype(BF16).astype(F32)
    t_out[...] = hi + pltpu.roll(tot - hi, 32, 1)


def whole(kernel, out_shape, name, *args):
    return pl.pallas_call(
        kernel,
        out_shape=out_shape,
        compiler_params=pltpu.CompilerParams(vmem_limit_bytes=VMEM_LIMIT),
        cost_estimate=CHEAP,
        name=name,
    )(*args)


def back_kernel(n_parts, nb, wide, tail, *refs):
    per, w_own, w_sib, tot = refs[:4]
    outs = refs[4:]
    j = pl.program_id(0)
    rows = w_own.shape[1]
    h = per.shape[0] // n_parts
    for i in range(wide):
        res = lax.dot_general(
            per[:, :rows], w_own[i], NN, preferred_element_type=F32
        ) + lax.dot_general(per[:, rows:], w_sib[i], NN, preferred_element_type=F32)
        at = pl.ds(pl.multiple_of(j * wide * KB + i * KB, KB), KB)
        for k, o in enumerate(outs):
            o[:, at] = res[k * h : (k + 1) * h, :].astype(BF16)
    if tail:

        @pl.when(j == nb - 1)
        def _():
            for k, o in enumerate(outs):
                o[:, nb * wide * KB :] = tot[k * h : (k + 1) * h, :].astype(BF16)


def back(per, w_own, w_sib, tot, quarter, n_parts):
    blocks, rows, _ = w_own.shape
    wide = 4
    nb = blocks // wide // 2
    off = quarter * nb
    h = per.shape[0] // n_parts
    tail = quarter == 0
    width = nb * wide * KB + (TAIL if tail else 0)
    return pl.pallas_call(
        functools.partial(back_kernel, n_parts, nb, wide, tail),
        grid=(nb,),
        in_specs=[
            full(per.shape),
            pl.BlockSpec((wide, rows, KB), lambda j: (off + j, 0, 0)),
            pl.BlockSpec((wide, rows, KB), lambda j: (off + j, 0, 0)),
            full(tot.shape),
        ],
        out_specs=[full((h, width))] * n_parts,
        out_shape=[jax.ShapeDtypeStruct((h, width), BF16)] * n_parts,
        compiler_params=params(),
        cost_estimate=CHEAP,
        name="back",
    )(per, w_own, w_sib, tot)


def add_tail(tail):
    tot = tail + pltpu.roll(tail, TAIL - 32, 1)
    lane = lax.broadcasted_iota(jnp.int32, tail.shape, 1)
    tot = jnp.where(lane < 32, tot, 0.0)
    hi = tot.astype(BF16).astype(F32)
    return hi + pltpu.roll(tot - hi, 32, 1)


def add_kernel(n, tail, *refs):
    out = refs[n]
    width = out.shape[1] - (TAIL if tail else 0)
    total = refs[0][...].astype(F32)
    for r in refs[1:n]:
        total = total + r[...].astype(F32)
    if tail:
        out[:, :width] = total[:, :width].astype(BF16)
        out[:, width:] = add_tail(total[:, width:]).astype(BF16)
    else:
        out[...] = total.astype(BF16)


def add(*arrays, tail):
    return whole(
        functools.partial(add_kernel, len(arrays), tail),
        jax.ShapeDtypeStruct(arrays[0].shape, BF16),
        "add",
        *arrays,
    )


def tie(value, *others):
    return lax.optimization_barrier((value, *others))[0]


def shards(images, classes, contrast, noise_weight, projections, proj_index):
    half = contrast.shape[1]
    quart = half // 2
    n_cls = contrast.shape[0]
    own_rows = projections.shape[1]
    h = 2 * own_rows
    me = lax.axis_index("img")
    core = (me % NC).astype(jnp.int32)
    chip = (me // NC).astype(jnp.int32)
    first = core == 0
    noise = noise_weight[None, :]

    mine = projections[0]
    low, high = mine[:, :half], mine[:, half:]
    got = to_core(jnp.where(first, high, low))
    kept = jnp.where(first, low, high)
    own_a, own_b = (
        jnp.where(
            first,
            jnp.concatenate([kept[:, cols], got[:, cols]], axis=0),
            jnp.concatenate([got[:, cols], kept[:, cols]], axis=0),
        )
        for cols in (slice(0, quart), slice(quart, half))
    )
    sib_classes = to_core(tie(classes, got))
    xm_a, xp_b, zz_a = to_xp(own_a), to_xm(own_b), to_z(tie(own_a, sib_classes))
    xm_b, xp_a = to_xp(own_b), to_xm(own_a)
    x2_a, x2_b = to_xp(xm_a), to_xm(xp_b)
    zz_b = to_z(tie(own_b, zz_a))
    fz_a, fz_b = tie(zz_a, x2_a, x2_b), tie(zz_b, x2_a, x2_b)
    zm_a, zp_a, z2_a = to_xp(fz_a), to_xm(fz_a), to_z(x2_a)

    ids = jnp.arange(n_cls, dtype=jnp.int32)[None, :]
    hot_own = (classes[:, None] == ids).astype(BF16)
    both_classes = jnp.concatenate([classes, sib_classes])
    hot = (both_classes[:, None] == ids).astype(F32)
    hot_wide = (both_classes[:, None] == jnp.arange(TAIL, dtype=jnp.int32)[None, :]).astype(BF16)
    hot3 = jnp.concatenate([hot_own] * 3, axis=1)
    w_own, give, quads = weigh(tie(core.reshape(1), own_a, sib_classes), images, hot3, contrast, noise)
    w_sib = to_core(tie(give, xm_a, xm_b, xp_a, xp_b, zz_a))
    zm_b, zp_b, z2_b = to_xp(tie(fz_b, w_sib)), to_xm(tie(fz_b, w_sib)), to_z(tie(x2_b, z2_a, w_sib))

    target = proj_index // h
    dz = (target // NX) ^ (chip // NX)
    dx = (target - chip) % NX
    near = jnp.where(dx == 0, 0, jnp.where(dx == 1, 1, jnp.where(dx == 3, 2, 4)))
    far = jnp.where(dx == 0, 3, jnp.where(dx == 1, 5, jnp.where(dx == 3, 6, 7)))
    rel = jnp.where(dz == 0, near, far) * h + proj_index % h
    block_width = 8 * h
    choose = (jnp.arange(block_width, dtype=jnp.int32)[:, None] == rel[None, :]).astype(F32)
    counts = jnp.sum(choose, axis=1, keepdims=True)

    table = (quads, hot)
    part = [own_a, xp_a, xm_a, zz_a, x2_a, zp_a, zm_a, z2_a]
    mine = score(part, w_own, w_sib, *table, 0, None)
    part = [own_b, xp_b, xm_b, zz_b, x2_b, zp_b, zm_b, z2_b]
    mine = score(part, w_own, w_sib, *table, 1, mine)
    stat_shape = jax.ShapeDtypeStruct((2, mine.shape[1]), F32)
    scores, stat = whole(
        stat_kernel,
        [jax.ShapeDtypeStruct(mine.shape, F32), stat_shape],
        "stat",
        mine,
        to_core(mine),
        counts,
    )
    stat = whole(
        merge_kernel,
        stat_shape,
        "merge",
        stat,
        lax.ppermute(stat, "ori", ori_perm(1, 0)),
    )
    stats = [stat] + [lax.ppermute(stat, "ori", ori_perm(0, y)) for y in range(1, 4)]
    per, tot, local = whole(
        functools.partial(chance_kernel, len(stats)),
        [
            jax.ShapeDtypeStruct((block_width, stat.shape[1]), BF16),
            jax.ShapeDtypeStruct((block_width, TAIL), F32),
            jax.ShapeDtypeStruct((block_width, stat.shape[1] // 2), F32),
        ],
        "chance",
        scores,
        counts,
        hot_wide,
        *stats,
    )
    log_weights = lax.dot_general(
        local, choose, (((0,), (0,)), ((), ())), precision=PRECISE
    )

    bo_a, bxp_a, bxm_a, bzz_a, bx2_a, bzp_a, bzm_a, bz2_a = back(
        per, w_own, w_sib, tot, 0, 8
    )
    bo_b, bxp_b, bxm_b, bzz_b, bx2_b, bzp_b, bzm_b, bz2_b = back(
        per, w_own, w_sib, tot, 1, 8
    )
    r_z2a, r_zma, r_zpa = to_z(bz2_a), to_xm(bzm_a), to_xp(bzp_a)
    r_z2b, r_zmb = to_z(bz2_b), to_xm(bzm_b)
    r_zpb = to_xp(tie(bzp_b, r_z2a))
    r_x2a = to_xm(tie(add(bx2_a, r_z2a, tail=True), r_zma))
    r_x2b = to_xp(tie(add(bx2_b, r_z2b, tail=False), r_zpa))
    r_zza = to_z(add(bzz_a, r_zma, r_zpa, tail=True))
    r_zzb = to_z(add(bzz_b, r_zmb, r_zpb, tail=False))
    r_xmb, r_xpa = to_xm(tie(bxm_b, r_zmb)), to_xp(tie(bxp_a, r_zpb))
    r_xma = to_xm(add(bxm_a, r_x2a, tail=True))
    r_xpb = to_xp(add(bxp_b, r_x2b, tail=False))
    fin_a = add(bo_a, r_xpa, r_xma, r_zza, tail=True)
    fin_b = add(bo_b, r_xpb, r_xmb, r_zzb, tail=False)

    fin = jnp.concatenate([fin_a[:, :quart], fin_b], axis=1)
    got = to_core(jnp.where(first, fin[own_rows:], fin[:own_rows]))
    kept = jnp.where(first, fin[:own_rows], fin[own_rows:])
    back_sums = jnp.where(
        first, jnp.concatenate([kept, got], axis=1), jnp.concatenate([got, kept], axis=1)
    )
    ends = fin_a[:, quart:].astype(F32)
    totals = ends[:, :n_cls] + ends[:, n_cls : 2 * n_cls]
    totals = jnp.where(first, totals[:own_rows], totals[own_rows:])
    contrast_mass = jnp.dot(totals, contrast * contrast, precision=PRECISE)
    return log_weights, back_sums[None], contrast_mass[None]


def solution(mesh):
    in_specs = (P("img", None), P("img"), P(), P(), P("ori", "img", None), P("ori"))
    out_specs = (P("img", "ori"), P("ori", "img", None), P("ori", "img", None))
    return jax.shard_map(shards, mesh=mesh, in_specs=in_specs, out_specs=out_specs, check_vma=False)
```

```python
import functools

import jax
import jax.numpy as jnp
from jax import lax
from jax.experimental import pallas as pl
from jax.experimental.pallas import tpu as pltpu
from jax.sharding import PartitionSpec as P

PRECISE = lax.Precision.HIGHEST
F32 = jnp.float32
BF16 = jnp.bfloat16
NX, NC = 4, 2
TAIL = 128
LANES = 256
KB = 1024
CHEAP = pl.CostEstimate(flops=1024, bytes_accessed=1024, transcendentals=0)
NT = (((1,), (1,)), ((), ()))
NN = (((1,), (0,)), ((), ()))
VMEM_LIMIT = 48 * 1024 * 1024


def img_perm(dz, dx, dc):
    pairs = []
    for z in range(2):
        for x in range(NX):
            for c in range(NC):
                src = (z * NX + x) * NC + c
                dst = ((z ^ dz) * NX + (x + dx) % NX) * NC + (c ^ dc)
                pairs.append((src, dst))
    return pairs


def ori_perm(dz, dy):
    return [(z * 4 + y, (z ^ dz) * 4 + (y + dy) % 4) for z in range(2) for y in range(4)]


def to_xp(v):
    return lax.ppermute(v, "img", img_perm(0, 1, 0))


def to_xm(v):
    return lax.ppermute(v, "img", img_perm(0, -1, 0))


def to_z(v):
    return lax.ppermute(v, "img", img_perm(1, 0, 0))


def to_core(v):
    return lax.ppermute(v, "img", img_perm(0, 0, 1))


def params(mib=48):
    return pltpu.CompilerParams(
        dimension_semantics=("arbitrary",), vmem_limit_bytes=mib * 1024 * 1024
    )


def full(shape):
    return pl.BlockSpec(shape, lambda j: (0,) * len(shape))


def weigh_kernel(core, keep, give, hot3, contrast, noise, keep_out, give_out, quad_out):
    amp = contrast[...] * noise[...]
    hq = 0.5 * contrast[...] * amp
    h1 = hq.astype(BF16)
    h2 = (hq - h1.astype(F32)).astype(BF16)
    quad_out[...] = jnp.concatenate([h1, h2], axis=0)
    a1 = amp.astype(BF16)
    rest = amp - a1.astype(F32)
    a2 = rest.astype(BF16)
    a3 = (rest - a2.astype(F32)).astype(BF16)
    table = jnp.concatenate([a1, a2, a3], axis=0)
    amplitude = lax.dot_general(hot3[...], table, NN, preferred_element_type=F32)
    for img, out in ((give, give_out), (keep, keep_out)):
        value = (img[...].astype(F32) * amplitude).astype(BF16)
        for i in range(out.shape[0]):
            out[i] = value[:, i * KB : (i + 1) * KB]


def weigh(core, images, hot3, contrast, noise):
    rows, cols = images.shape
    half = cols // 2
    wide = 4
    kb = wide * KB
    nb = half // kb
    n_cls = contrast.shape[0]
    return pl.pallas_call(
        weigh_kernel,
        grid_spec=pltpu.PrefetchScalarGridSpec(
            num_scalar_prefetch=1,
            grid=(nb,),
            in_specs=[
                pl.BlockSpec((rows, kb), lambda j, s: (0, s[0] * nb + j)),
                pl.BlockSpec((rows, kb), lambda j, s: (0, (1 - s[0]) * nb + j)),
                pl.BlockSpec(hot3.shape, lambda j, s: (0, 0)),
                pl.BlockSpec((n_cls, kb), lambda j, s: (0, j)),
                pl.BlockSpec((1, kb), lambda j, s: (0, j)),
            ],
            out_specs=[
                pl.BlockSpec((wide, rows, KB), lambda j, s: (j, 0, 0)),
                pl.BlockSpec((wide, rows, KB), lambda j, s: (j, 0, 0)),
                pl.BlockSpec((2 * n_cls, kb), lambda j, s: (0, j)),
            ],
        ),
        out_shape=[
            jax.ShapeDtypeStruct((half // KB, rows, KB), BF16),
            jax.ShapeDtypeStruct((half // KB, rows, KB), BF16),
            jax.ShapeDtypeStruct((2 * n_cls, half), BF16),
        ],
        compiler_params=params(56),
        cost_estimate=CHEAP,
        name="weigh",
    )(core, images, images, hot3, contrast, noise)


def score_kernel(n_parts, has_acc, nb, wide, *refs):
    parts = refs[:n_parts]
    w_own, w_sib, quads, hot = refs[n_parts : n_parts + 4]
    pos = n_parts + 4
    acc_in = refs[pos] if has_acc else None
    out, acc, qacc = refs[pos + has_acc :]
    j = pl.program_id(0)

    @pl.when(j == 0)
    def _():
        acc[...] = jnp.zeros_like(acc)
        qacc[...] = jnp.zeros_like(qacc)

    rows = w_own.shape[1]
    own, sib, quad = None, None, None
    for i in range(wide):
        cols = slice(i * KB, (i + 1) * KB)
        pieces = [r[:, cols].astype(F32) for r in parts]
        used = sum(p.shape[0] for p in pieces)
        pieces.append(jnp.zeros((LANES - used, KB), F32))
        p32 = jnp.concatenate(pieces, axis=0)
        pb = p32.astype(BF16)
        d_own = lax.dot_general(w_own[i], pb, NT, preferred_element_type=F32)
        d_sib = lax.dot_general(w_sib[i], pb, NT, preferred_element_type=F32)
        sq = p32 * p32
        hi = sq.astype(BF16)
        lo = (sq - hi.astype(F32)).astype(BF16)
        hh = quads[:, cols]
        d_quad = lax.dot_general(hh, hi, NT, preferred_element_type=F32) + lax.dot_general(
            hh, lo, NT, preferred_element_type=F32
        )
        own = d_own if own is None else own + d_own
        sib = d_sib if sib is None else sib + d_sib
        quad = d_quad if quad is None else quad + d_quad
    acc[:rows, :] += own
    acc[rows:, :] += sib
    qacc[...] += quad

    @pl.when(j == nb - 1)
    def _():
        n_cls = qacc.shape[0] // 2
        q = qacc[:n_cls, :] + qacc[n_cls:, :]
        total = acc[...] - jnp.dot(hot[...], q, precision=PRECISE, preferred_element_type=F32)
        turned = jnp.transpose(total)[:used, :]
        if has_acc:
            turned = turned + acc_in[...]
        out[...] = turned


def score(parts, w_own, w_sib, quads, hot, quarter, acc_in):
    part_rows = parts[0].shape[0]
    rows = w_own.shape[1]
    wide = 4
    kb = wide * KB
    nb = w_own.shape[0] // wide // 2
    used = part_rows * len(parts)
    off = quarter * nb
    in_specs = []
    for p in parts:
        at = off if p.shape[1] > nb * kb else 0
        in_specs.append(pl.BlockSpec((part_rows, kb), lambda j, at=at: (0, at + j)))
    in_specs += [
        pl.BlockSpec((wide, rows, KB), lambda j: (off + j, 0, 0)),
        pl.BlockSpec((wide, rows, KB), lambda j: (off + j, 0, 0)),
        pl.BlockSpec((quads.shape[0], kb), lambda j: (0, off + j)),
        full(hot.shape),
    ]
    quads = pltpu.with_memory_space_constraint(quads, pltpu.HBM)
    args = [*parts, w_own, w_sib, quads, hot]
    if acc_in is not None:
        in_specs.append(full((used, 2 * rows)))
        args.append(acc_in)
    return pl.pallas_call(
        functools.partial(score_kernel, len(parts), acc_in is not None, nb, wide),
        grid=(nb,),
        in_specs=in_specs,
        out_specs=full((used, 2 * rows)),
        out_shape=jax.ShapeDtypeStruct((used, 2 * rows), F32),
        scratch_shapes=[
            pltpu.VMEM((2 * rows, LANES), F32),
            pltpu.VMEM((quads.shape[0], LANES), F32),
        ],
        compiler_params=params(),
        cost_estimate=CHEAP,
        name="score",
    )(*args)


def stat_kernel(mine, recv, cnt, out, st_out):
    rows = mine.shape[1] // 2
    r = recv[...]
    total = mine[...] + jnp.concatenate([r[:, rows:], r[:, :rows]], axis=1)
    out[...] = total
    peak = jnp.max(total, axis=0, keepdims=True)
    st_out[0:1, :] = peak
    st_out[1:2, :] = jnp.sum(jnp.exp(total - peak) * cnt[...], axis=0, keepdims=True)


def merge(stats):
    peak = stats[0][0:1, :]
    for s in stats[1:]:
        peak = jnp.maximum(peak, s[0:1, :])
    mass = jnp.zeros_like(peak)
    for s in stats:
        mass = mass + s[1:2, :] * jnp.exp(s[0:1, :] - peak)
    return peak, mass


def merge_kernel(*refs):
    peak, mass = merge(refs[:-1])
    refs[-1][0:1, :] = peak
    refs[-1][1:2, :] = mass


def chance_kernel(n, *refs):
    scores, cnt, hot = refs[:3]
    p_out, t_out, l_out = refs[3 + n :]
    peak, mass = merge(refs[3 : 3 + n])
    shift = peak + jnp.log(mass)
    own = l_out.shape[1]
    lw = scores[...] - shift
    l_out[...] = lw[:, :own]
    chance = jnp.exp(lw).astype(BF16).astype(F32)
    per = (chance * cnt[...]).astype(BF16)
    p_out[...] = per
    tot = jnp.dot(per, hot[...], preferred_element_type=F32)
    hi = tot.astype(BF16).astype(F32)
    t_out[...] = hi + pltpu.roll(tot - hi, 32, 1)


def whole(kernel, out_shape, name, *args):
    return pl.pallas_call(
        kernel,
        out_shape=out_shape,
        compiler_params=pltpu.CompilerParams(vmem_limit_bytes=VMEM_LIMIT),
        cost_estimate=CHEAP,
        name=name,
    )(*args)


def back_kernel(n_parts, nb, wide, tail, *refs):
    per, w_own, w_sib, tot = refs[:4]
    outs = refs[4:]
    j = pl.program_id(0)
    rows = w_own.shape[1]
    h = per.shape[0] // n_parts
    for i in range(wide):
        res = lax.dot_general(
            per[:, :rows], w_own[i], NN, preferred_element_type=F32
        ) + lax.dot_general(per[:, rows:], w_sib[i], NN, preferred_element_type=F32)
        at = pl.ds(pl.multiple_of(j * wide * KB + i * KB, KB), KB)
        for k, o in enumerate(outs):
            o[:, at] = res[k * h : (k + 1) * h, :].astype(BF16)
    if tail:

        @pl.when(j == nb - 1)
        def _():
            for k, o in enumerate(outs):
                o[:, nb * wide * KB :] = tot[k * h : (k + 1) * h, :].astype(BF16)


def back(per, w_own, w_sib, tot, quarter, n_parts):
    blocks, rows, _ = w_own.shape
    wide = 4
    nb = blocks // wide // 2
    off = quarter * nb
    h = per.shape[0] // n_parts
    tail = quarter == 0
    width = nb * wide * KB + (TAIL if tail else 0)
    return pl.pallas_call(
        functools.partial(back_kernel, n_parts, nb, wide, tail),
        grid=(nb,),
        in_specs=[
            full(per.shape),
            pl.BlockSpec((wide, rows, KB), lambda j: (off + j, 0, 0)),
            pl.BlockSpec((wide, rows, KB), lambda j: (off + j, 0, 0)),
            full(tot.shape),
        ],
        out_specs=[full((h, width))] * n_parts,
        out_shape=[jax.ShapeDtypeStruct((h, width), BF16)] * n_parts,
        compiler_params=params(),
        cost_estimate=CHEAP,
        name="back",
    )(per, w_own, w_sib, tot)


def add_tail(tail):
    tot = tail + pltpu.roll(tail, TAIL - 32, 1)
    lane = lax.broadcasted_iota(jnp.int32, tail.shape, 1)
    tot = jnp.where(lane < 32, tot, 0.0)
    hi = tot.astype(BF16).astype(F32)
    return hi + pltpu.roll(tot - hi, 32, 1)


def add_kernel(n, tail, *refs):
    out = refs[n]
    width = out.shape[1] - (TAIL if tail else 0)
    total = refs[0][...].astype(F32)
    for r in refs[1:n]:
        total = total + r[...].astype(F32)
    if tail:
        out[:, :width] = total[:, :width].astype(BF16)
        out[:, width:] = add_tail(total[:, width:]).astype(BF16)
    else:
        out[...] = total.astype(BF16)


def add(*arrays, tail):
    return whole(
        functools.partial(add_kernel, len(arrays), tail),
        jax.ShapeDtypeStruct(arrays[0].shape, BF16),
        "add",
        *arrays,
    )


def tie(value, *others):
    return lax.optimization_barrier((value, *others))[0]


def shards(images, classes, contrast, noise_weight, projections, proj_index):
    half = contrast.shape[1]
    quart = half // 2
    n_cls = contrast.shape[0]
    own_rows = projections.shape[1]
    h = 2 * own_rows
    me = lax.axis_index("img")
    core = (me % NC).astype(jnp.int32)
    chip = (me // NC).astype(jnp.int32)
    first = core == 0
    noise = noise_weight[None, :]

    mine = projections[0]
    low, high = mine[:, :half], mine[:, half:]
    got = to_core(jnp.where(first, high, low))
    ids = jnp.arange(n_cls, dtype=jnp.int32)[None, :]
    hot_own = (classes[:, None] == ids).astype(BF16)
    hot3 = jnp.concatenate([hot_own] * 3, axis=1)
    kept = tie(jnp.where(first, low, high), hot3)
    own_a, own_b = (
        jnp.where(
            first,
            jnp.concatenate([kept[:, cols], got[:, cols]], axis=0),
            jnp.concatenate([got[:, cols], kept[:, cols]], axis=0),
        )
        for cols in (slice(0, quart), slice(quart, half))
    )
    sib_classes = to_core(tie(classes, got))
    xm_a, xp_b, zz_a = to_xp(own_a), to_xm(own_b), to_z(tie(own_a, sib_classes))
    xm_b, xp_a = to_xp(own_b), to_xm(own_a)
    x2_a, x2_b = to_xp(xm_a), to_xm(xp_b)
    zz_b = to_z(tie(own_b, zz_a))
    fz_a, fz_b = tie(zz_a, x2_a, x2_b), tie(zz_b, x2_a, x2_b)
    zm_a, zp_a, z2_a = to_xp(fz_a), to_xm(fz_a), to_z(x2_a)

    both_classes = jnp.concatenate([classes, sib_classes])
    hot = (both_classes[:, None] == ids).astype(F32)
    hot_wide = (both_classes[:, None] == jnp.arange(TAIL, dtype=jnp.int32)[None, :]).astype(BF16)
    w_own, give, quads = weigh(tie(core.reshape(1), own_a, sib_classes), images, hot3, contrast, noise)
    w_sib = to_core(tie(give, xm_a, xm_b, xp_a, xp_b, zz_a))
    zm_b, zp_b, z2_b = to_xp(tie(fz_b, w_sib)), to_xm(tie(fz_b, w_sib)), to_z(tie(x2_b, z2_a, w_sib))

    target = proj_index // h
    dz = (target // NX) ^ (chip // NX)
    dx = (target - chip) % NX
    near = jnp.where(dx == 0, 0, jnp.where(dx == 1, 1, jnp.where(dx == 3, 2, 4)))
    far = jnp.where(dx == 0, 3, jnp.where(dx == 1, 5, jnp.where(dx == 3, 6, 7)))
    rel = jnp.where(dz == 0, near, far) * h + proj_index % h
    block_width = 8 * h
    choose = (jnp.arange(block_width, dtype=jnp.int32)[:, None] == rel[None, :]).astype(F32)
    counts = jnp.sum(choose, axis=1, keepdims=True)

    table = (quads, hot)
    part = [own_a, xp_a, xm_a, zz_a, x2_a, zp_a, zm_a, z2_a]
    mine = score(part, w_own, w_sib, *table, 0, None)
    part = [own_b, xp_b, xm_b, zz_b, x2_b, zp_b, zm_b, z2_b]
    mine = score(part, w_own, w_sib, *table, 1, mine)
    stat_shape = jax.ShapeDtypeStruct((2, mine.shape[1]), F32)
    scores, stat = whole(
        stat_kernel,
        [jax.ShapeDtypeStruct(mine.shape, F32), stat_shape],
        "stat",
        mine,
        to_core(mine),
        counts,
    )
    stat = whole(
        merge_kernel,
        stat_shape,
        "merge",
        stat,
        lax.ppermute(stat, "ori", ori_perm(1, 0)),
    )
    stats = [stat] + [lax.ppermute(stat, "ori", ori_perm(0, y)) for y in range(1, 4)]
    per, tot, local = whole(
        functools.partial(chance_kernel, len(stats)),
        [
            jax.ShapeDtypeStruct((block_width, stat.shape[1]), BF16),
            jax.ShapeDtypeStruct((block_width, TAIL), F32),
            jax.ShapeDtypeStruct((block_width, stat.shape[1] // 2), F32),
        ],
        "chance",
        scores,
        counts,
        hot_wide,
        *stats,
    )
    log_weights = lax.dot_general(
        local, choose, (((0,), (0,)), ((), ())), precision=PRECISE
    )

    bo_a, bxp_a, bxm_a, bzz_a, bx2_a, bzp_a, bzm_a, bz2_a = back(
        per, w_own, w_sib, tot, 0, 8
    )
    bo_b, bxp_b, bxm_b, bzz_b, bx2_b, bzp_b, bzm_b, bz2_b = back(
        per, w_own, w_sib, tot, 1, 8
    )
    r_z2a, r_zma, r_zpa = to_z(bz2_a), to_xm(bzm_a), to_xp(bzp_a)
    r_z2b, r_zmb = to_z(bz2_b), to_xm(bzm_b)
    r_zpb = to_xp(tie(bzp_b, r_z2a))
    r_x2a = to_xm(tie(add(bx2_a, r_z2a, tail=True), r_zma))
    r_x2b = to_xp(tie(add(bx2_b, r_z2b, tail=False), r_zpa))
    r_zza = to_z(add(bzz_a, r_zma, r_zpa, tail=True))
    r_zzb = to_z(add(bzz_b, r_zmb, r_zpb, tail=False))
    r_xmb, r_xpa = to_xm(tie(bxm_b, r_zmb)), to_xp(tie(bxp_a, r_zpb))
    r_xma = to_xm(add(bxm_a, r_x2a, tail=True))
    r_xpb = to_xp(add(bxp_b, r_x2b, tail=False))
    fin_a = add(bo_a, r_xpa, r_xma, r_zza, tail=True)
    fin_b = add(bo_b, r_xpb, r_xmb, r_zzb, tail=False)

    fin = jnp.concatenate([fin_a[:, :quart], fin_b], axis=1)
    got = to_core(jnp.where(first, fin[own_rows:], fin[:own_rows]))
    kept = jnp.where(first, fin[:own_rows], fin[own_rows:])
    back_sums = jnp.where(
        first, jnp.concatenate([kept, got], axis=1), jnp.concatenate([got, kept], axis=1)
    )
    ends = fin_a[:, quart:].astype(F32)
    totals = ends[:, :n_cls] + ends[:, n_cls : 2 * n_cls]
    totals = jnp.where(first, totals[:own_rows], totals[own_rows:])
    contrast_mass = jnp.dot(totals, contrast * contrast, precision=PRECISE)
    return log_weights, back_sums[None], contrast_mass[None]


def solution(mesh):
    in_specs = (P("img", None), P("img"), P(), P(), P("ori", "img", None), P("ori"))
    out_specs = (P("img", "ori"), P("ori", "img", None), P("ori", "img", None))
    return jax.shard_map(shards, mesh=mesh, in_specs=in_specs, out_specs=out_specs, check_vma=False)
```
